32 devices in a mesh: grp: 4 (over y, x), blk: 8 (over z, core).
Axes of the slice: x: 2, y: 2, z: 4, core: 2. Of those that a mesh axis runs over, the one named last changes fastest.
Arguments:
- residual_in: bfloat16 [256, 16384], P('grp', 'blk'), may hold values from -6 to 6
- queries: bfloat16 [256, 16384], P('grp')
- key_cache: bfloat16 [256, 8, 64, 128], P('grp', 'blk')
- value_cache: bfloat16 [256, 8, 64, 128], P('grp', 'blk'), may hold values from -6 to 6
- key_new: bfloat16 [256, 1024], P('grp'), may hold values from -6 to 6
- value_new: bfloat16 [256, 1024], P('grp'), may hold values from -6 to 6
- lengths: int32 [256], P('grp'), may hold values from 2 to 64, as said below
- ffn_gain: bfloat16 [16384], P('blk'), may hold values from 0.099609375 to 1.8984375
- gate_weight: bfloat16 [16384, 26624], P('blk', 'grp'), may hold values from -0.046875 to 0.046875
- up_weight: bfloat16 [16384, 26624], P('blk', 'grp'), may hold values from -0.046875 to 0.046875
- down_weight: bfloat16 [26624, 16384], P('grp', 'blk'), may hold values from -0.0390625 to 0.0390625
Outputs:
- layer_out: float32 [256, 16384], P('grp', 'blk')
The draws below stay inside these ranges and needn't reach their ends.
Inputs may be any that keep to these rules, and one draw needn't show every extreme that they name: `lengths`: every sequence has at least two valid cache positions, and some sequence fills all 64.
All inputs are finite; a program needn't handle non-finite values.
Results may differ from the reference program's by a relative error of at most 0.0075.
Values may be sent and summed in bfloat16 or wider, within the bound.
No kernel may reach another device: no remote copies, remote signals or barrier semaphores. Data moves between devices by JAX's collectives and lax.ppermute only.
A program may use at most 192 MiB of HBM per device.

```python
import math
import jax
import jax.numpy as jnp
from jax import lax

D = 16384
HEADS = 128
KV_HEADS = 8
HD = 128
FF = 26624
CTX_Q = 64
B = 256
SPLIT = 1
CTX = 64
N_BLK = 8


def cache_keys(key):
    return jax.random.normal(jax.random.fold_in(key, 11), (B, KV_HEADS * SPLIT, CTX_Q, HD), jnp.float32)


def draw_key_cache(key, part):
    shared = cache_keys(key)
    return shared.astype(jnp.bfloat16)


def draw_queries(key, part):
    key = jax.random.fold_in(key, 5)
    jitter = jax.random.normal(key, (B, HEADS, HD), jnp.float32)
    values = 2.0 * jitter
    return values.reshape(B, HEADS * HD).astype(jnp.bfloat16)


def draw_lengths(key, part):
    key = jax.random.fold_in(key, 9)
    drawn = jax.random.randint(key, (B,), 2, CTX + 1, dtype=jnp.int32)
    return drawn.at[0].set(CTX).astype(jnp.int32)


def levels(stream_key, shape, shards, low, top_value):
    gain = 1.0
    for position, shards_of in shards:
        draws = jax.random.uniform(jax.random.fold_in(jax.random.fold_in(stream_key, 6), position), (shards_of,), jnp.float32, low / len(shards), top_value / len(shards))
        gain = gain * jnp.repeat(jnp.exp(draws), shape[position] // shards_of).reshape((-1,) + (1,) * (len(shape) - 1 - position))
    return gain


def noise(rng, dims, scale, limit, split=(), kind=jnp.bfloat16):
    array = jax.random.normal(rng, dims, jnp.float32) * scale
    if len(split) > 0:
        array = levels(rng, dims, split, -0.22, 0.18) * array
    return jnp.clip(array, min=-limit, max=limit).astype(kind)


def setup_inputs(seed: int = 0) -> dict:
    splits = jax.random.split(jax.random.key(seed), 12)
    return {
        "residual_in": noise(splits[0], (B, D), 0.5, 6.0, ((0, 4), (1, 8))),
        "queries": draw_queries(jax.random.fold_in(splits[11], 71), 0),
        "key_cache": draw_key_cache(jax.random.fold_in(splits[11], 71), 0),
        "value_cache": noise(splits[3], (B, KV_HEADS * SPLIT, CTX_Q, HD), 1.0, 6.0, ((0, 4), (1, 8))),
        "key_new": noise(splits[4], (B, KV_HEADS * HD), 1.0, 6.0, ((0, 4),)),
        "value_new": noise(splits[5], (B, KV_HEADS * HD), 1.0, 6.0, ((0, 4),)),
        "lengths": draw_lengths(jax.random.fold_in(splits[11], 71), 0),
        "ffn_gain": jnp.clip(1.0 + 0.18 * jax.random.normal(splits[7], (D,), jnp.float32), 0.099609375, 1.8984375).astype(jnp.bfloat16),
        "gate_weight": noise(splits[8], (D, FF), D ** -0.5, 0.046875, ((0, 8), (1, 4))),
        "up_weight": noise(splits[9], (D, FF), D ** -0.5, 0.046875, ((0, 8), (1, 4))),
        "down_weight": noise(splits[10], (FF, D), FF ** -0.5, 0.0390625, ((0, 4), (1, 8))),
    }


def attend_one(operands):
    query_row, key_rows, value_rows, key_fresh, value_fresh, length = operands
    quarters = N_BLK // KV_HEADS
    per_kv = HEADS // KV_HEADS
    score_scale = 1.0 / math.sqrt(HD)
    query_heads = query_row.astype(jnp.float32).reshape(KV_HEADS, per_kv, HD)
    keys_all = key_rows.astype(jnp.float32).reshape(KV_HEADS, quarters * CTX_Q, HD)
    values_all = value_rows.astype(jnp.float32).reshape(KV_HEADS, quarters * CTX_Q, HD)
    places = jnp.arange(quarters * CTX_Q, dtype=jnp.int32)
    usable = (places < length)[None, None, :]
    scores = jnp.einsum('khd,kpd->khp', query_heads, keys_all) * score_scale
    fresh_key = key_fresh.astype(jnp.float32).reshape(KV_HEADS, HD)
    fresh_value = value_fresh.astype(jnp.float32).reshape(KV_HEADS, 1, HD)
    fresh = jnp.einsum('khd,kd->kh', query_heads, fresh_key) * score_scale
    largest = jnp.maximum(lax.optimization_barrier(jnp.max(jnp.where(usable, scores, -jnp.inf), axis=2)), fresh)
    weights = jnp.where(usable, jnp.exp(scores - largest[..., None]), 0.0)
    fresh_weight = jnp.exp(fresh - largest)
    totals = lax.optimization_barrier(jnp.sum(weights, axis=2)) + fresh_weight
    weighted = jnp.einsum('khp,kpd->khd', weights, values_all) + fresh_weight[..., None] * fresh_value
    return (weighted / totals[..., None]).reshape(HEADS * HD)

def reference(residual_in, queries, key_cache, value_cache, key_new, value_new, lengths, ffn_gain, gate_weight, up_weight, down_weight):
    attention = lax.map(attend_one, (queries, key_cache, value_cache, key_new, value_new, lengths))
    wide = residual_in.astype(jnp.float32) + attention
    mean_square = lax.optimization_barrier(jnp.mean(wide * wide, axis=1))
    normed = (wide * ffn_gain.astype(jnp.float32)[None, :] * lax.rsqrt(mean_square + 1e-05)[:, None]).astype(jnp.bfloat16)
    gate = jnp.dot(normed, gate_weight, preferred_element_type=jnp.float32)
    up_part = jnp.dot(normed, up_weight, preferred_element_type=jnp.float32)
    hidden = (jax.nn.silu(gate) * up_part).astype(jnp.bfloat16)
    down = jnp.dot(hidden, down_weight, preferred_element_type=jnp.float32)
    return wide + down
```

```python
import functools
import math

import jax
import jax.numpy as jnp
from jax import lax
from jax.experimental import pallas as pl
from jax.experimental.pallas import tpu as pltpu
from jax.sharding import PartitionSpec as P

D = 16384
HEADS = 128
KV_HEADS = 8
UNIT = 256
CHUNKS = 4
VMEM = 48 * 1024 * 1024


def partner(x, axis, distance):
    return lax.ppermute(x, axis, [(i, i ^ distance) for i in range(lax.axis_size(axis))])


def along_line(x, step):
    chips = lax.axis_size("blk") // 2
    hops = [(step - 1, step), (chips - step, chips - step - 1)]
    return lax.ppermute(x, "blk", [(2 * a + c, 2 * b + c) for a, b in hops for c in range(2)])


def gate_up_kernel(n_blocks, place_ref, *refs):
    blocks, (gate_ref, up_ref, first_ref, second_ref, send_ref, x_ref) = (
        refs[:n_blocks],
        refs[n_blocks:],
    )
    rows = blocks[0].shape[0]
    quarter = first_ref.shape[1]

    @pl.when(pl.program_id(0) == 0)
    def _():
        for i, block in enumerate(blocks):
            x_ref[pl.ds(pl.multiple_of(place_ref[i] * rows, rows), rows), :] = block[...]

    for i, weight in enumerate((gate_ref, up_ref)):
        y = jnp.dot(x_ref[...], weight[...], preferred_element_type=jnp.float32)
        first_ref[i] = y[:quarter]
        second_ref[i] = y[quarter : 2 * quarter]
        send_ref[i] = y[2 * quarter :].astype(jnp.bfloat16)


def gate_up(place, blocks, gate_weight, up_weight, start, units):
    rows, depth = blocks[0].shape
    total = rows * len(blocks)
    quarter = total // 4
    cols = units * UNIT
    weight_spec = pl.BlockSpec((depth, UNIT), lambda i: (0, start + i))
    return pl.pallas_call(
        functools.partial(gate_up_kernel, len(blocks)),
        grid=(units,),
        in_specs=[pl.BlockSpec(memory_space=pltpu.SMEM)]
        + [pl.BlockSpec((rows, depth), lambda i: (0, 0))] * len(blocks)
        + [weight_spec, weight_spec],
        out_specs=[
            pl.BlockSpec((2, quarter, UNIT), lambda i: (0, 0, i)),
            pl.BlockSpec((2, quarter, UNIT), lambda i: (0, 0, i)),
            pl.BlockSpec((2, 2 * quarter, UNIT), lambda i: (0, 0, i)),
        ],
        out_shape=[
            jax.ShapeDtypeStruct((2, quarter, cols), jnp.float32),
            jax.ShapeDtypeStruct((2, quarter, cols), jnp.float32),
            jax.ShapeDtypeStruct((2, 2 * quarter, cols), jnp.bfloat16),
        ],
        scratch_shapes=[pltpu.VMEM((total, depth), jnp.bfloat16)],
        compiler_params=pltpu.CompilerParams(vmem_limit_bytes=VMEM),
        cost_estimate=pl.CostEstimate(
            flops=4 * total * depth * cols,
            bytes_accessed=4 * depth * cols + 2 * total * depth + 12 * total * cols,
            transcendentals=0,
        ),
    )(place, *blocks, gate_weight, up_weight)


def down_kernel(has_total, *refs):
    parts, weight_ref, rest = refs[:4], refs[4], refs[5:]
    out_ref = rest[-1]
    x = jnp.concatenate([part[...] for part in parts], axis=0)
    y = jnp.dot(x, weight_ref[...], preferred_element_type=jnp.float32)

    @pl.when(pl.program_id(0) == 0)
    def _():
        if has_total:
            out_ref[...] = rest[0][...] + y
        else:
            out_ref[...] = y

    @pl.when(pl.program_id(0) > 0)
    def _():
        out_ref[...] += y


def down(parts, weight, total, start, units):
    quarter = parts[0].shape[0]
    width = weight.shape[1]
    out = pl.BlockSpec((4 * quarter, width), lambda i: (0, 0))
    has_total = total is not None
    return pl.pallas_call(
        functools.partial(down_kernel, has_total),
        grid=(units,),
        in_specs=[pl.BlockSpec((quarter, UNIT), lambda i: (0, i))] * 4
        + [pl.BlockSpec((UNIT, width), lambda i: (start + i, 0))]
        + [out] * has_total,
        out_specs=out,
        out_shape=jax.ShapeDtypeStruct((4 * quarter, width), jnp.float32),
        input_output_aliases={5: 0} if has_total else {},
        compiler_params=pltpu.CompilerParams(vmem_limit_bytes=VMEM),
        cost_estimate=pl.CostEstimate(
            flops=8 * quarter * units * UNIT * width,
            bytes_accessed=2 * units * UNIT * width + 32 * quarter * width,
            transcendentals=0,
        ),
    )(*parts, weight, *([total] if has_total else []))


def attend(residual_in, queries, key_cache, value_cache, key_new, value_new, lengths):
    cycle_size = lax.axis_size("blk")
    quarters = cycle_size // KV_HEADS
    per_kv = HEADS // KV_HEADS
    own_heads = HEADS // cycle_size
    head_size = key_cache.shape[3]
    seq_rows = residual_in.shape[0]
    positions_here = key_cache.shape[2]
    blk_index = lax.axis_index("blk")
    kv_head = blk_index // quarters
    quarter = blk_index % quarters
    score_scale = 1.0 / math.sqrt(head_size)
    group_queries = lax.dynamic_slice_in_dim(
        queries, kv_head * per_kv * head_size, per_kv * head_size, 1
    )
    group_queries = group_queries.astype(jnp.float32).reshape(seq_rows, per_kv, head_size)
    fresh_key = lax.dynamic_slice_in_dim(key_new, kv_head * head_size, head_size, 1).astype(
        jnp.float32
    )
    fresh_value = lax.dynamic_slice_in_dim(value_new, kv_head * head_size, head_size, 1).astype(
        jnp.float32
    )
    keys_here = key_cache[:, 0].astype(jnp.float32)
    values_here = value_cache[:, 0].astype(jnp.float32)
    scores = jnp.einsum("shd,spd->shp", group_queries, keys_here) * score_scale
    fresh_scores = jnp.einsum("shd,sd->sh", group_queries, fresh_key) * score_scale
    places = quarter * positions_here + jnp.arange(positions_here, dtype=jnp.int32)
    usable = (places[None, :] < lengths[:, None])[:, None, :]
    with_fresh = quarter == 0
    largest = jnp.maximum(
        jnp.max(jnp.where(usable, scores, -1e30), axis=2),
        jnp.where(with_fresh, fresh_scores, -1e30),
    )
    weights = jnp.where(usable, jnp.exp(scores - largest[..., None]), 0.0)
    fresh_weight = jnp.where(with_fresh, jnp.exp(fresh_scores - largest), 0.0)
    totals = jnp.sum(weights, axis=2) + fresh_weight
    weighted = (
        jnp.einsum("shp,spd->shd", weights, values_here)
        + fresh_weight[..., None] * fresh_value[:, None, :]
    )
    for bit_number in range(quarters.bit_length() - 1):
        peer_max, peer_total, peer_weighted = partner(
            (largest, totals, weighted), "blk", 1 << bit_number
        )
        merged = jnp.maximum(largest, peer_max)
        mine_factor = jnp.exp(largest - merged)
        peer_factor = jnp.exp(peer_max - merged)
        totals = totals * mine_factor + peer_total * peer_factor
        weighted = weighted * mine_factor[..., None] + peer_weighted * peer_factor[..., None]
        largest = merged
    attention = weighted / totals[..., None]
    own_output = lax.dynamic_slice_in_dim(attention, quarter * own_heads, own_heads, 1).reshape(
        seq_rows, own_heads * head_size
    )
    return residual_in.astype(jnp.float32) + own_output


def on_device(
    residual_in,
    queries,
    key_cache,
    value_cache,
    key_new,
    value_new,
    lengths,
    ffn_gain,
    gate_weight,
    up_weight,
    down_weight,
):
    groups = lax.axis_size("grp")
    group = lax.axis_index("grp")
    chips = lax.axis_size("blk") // 2
    chip, core = lax.axis_index("blk") // 2, lax.axis_index("blk") % 2
    rows = residual_in.shape[0]
    per_quarter = groups // 4
    quarter = per_quarter * rows

    wide = attend(residual_in, queries, key_cache, value_cache, key_new, value_new, lengths)

    tokens = (wide * ffn_gain.astype(jnp.float32)[None, :]).astype(jnp.bfloat16)
    blocks = [tokens] + [partner(tokens, "grp", i) for i in range(1, groups)]

    squares = jnp.sum(wide * wide, axis=1)
    for bit_number in range(lax.axis_size("blk").bit_length() - 1):
        squares = squares + partner(squares, "blk", 1 << bit_number)
    squares = jnp.stack([squares] + [partner(squares, "grp", i) for i in range(1, groups)])

    lead = 2 * core + jnp.where(chip >= chips // 2, 0, 1)
    turn = group ^ (lead * per_quarter)
    place = jnp.arange(groups, dtype=jnp.int32) ^ turn
    last_rows = jnp.arange(per_quarter, dtype=jnp.int32) + per_quarter
    inverse = lax.rsqrt(squares[last_rows ^ turn].reshape(quarter) / D + 1e-05)[:, None]

    n_units = gate_weight.shape[1] // UNIT
    edges = [n_units * i // CHUNKS for i in range(CHUNKS + 1)]
    f32 = jnp.float32
    total = None
    for start, stop in zip(edges[:-1], edges[1:]):
        first, second, send = gate_up(place, blocks, gate_weight, up_weight, start, stop - start)
        other = partner(send, "blk", 1)
        first = first + other[:, :quarter].astype(f32)
        second = second + other[:, quarter:].astype(f32)
        flow = None
        for step in range(1, chips):
            own = first if step <= chips // 2 else second
            flow = own if flow is None else own + flow.astype(f32)
            flow = along_line(flow.astype(jnp.bfloat16), step)
        sums = second + flow.astype(f32)
        gate, up_part = sums[0] * inverse, sums[1] * inverse
        hidden = (jax.nn.silu(gate) * up_part).astype(jnp.bfloat16)
        halves = [hidden, None]
        for step in range(1, chips):
            hidden = along_line(hidden, step)
            half = step // (chips // 2)
            here = (chip == step) | (chip == chips - 1 - step)
            halves[half] = hidden if halves[half] is None else jnp.where(here, hidden, halves[half])
        halves = [halves[1], halves[0]]
        theirs = [partner(half, "blk", 1) for half in halves]
        total = down(halves + theirs, down_weight, total, start, stop - start)

    terms = total.reshape(groups, rows, -1)
    own = lax.dynamic_index_in_dim(terms, turn, 0, keepdims=False)
    out = wide + own
    for i in range(1, groups):
        term = lax.dynamic_index_in_dim(terms, turn ^ i, 0, keepdims=False)
        out = out + partner(term.astype(jnp.bfloat16), "grp", i).astype(f32)
    return out


def solution(mesh):
    in_specs = (
        P("grp", "blk"),
        P("grp", None),
        P("grp", "blk", None, None),
        P("grp", "blk", None, None),
        P("grp", None),
        P("grp", None),
        P("grp"),
        P("blk"),
        P("blk", "grp"),
        P("blk", "grp"),
        P("grp", "blk"),
    )
    out_specs = P("grp", "blk")
    return jax.shard_map(
        on_device, mesh=mesh, in_specs=in_specs, out_specs=out_specs, check_vma=False
    )
```

```python
import functools
import math

import jax
import jax.numpy as jnp
from jax import lax
from jax.experimental import pallas as pl
from jax.experimental.pallas import tpu as pltpu
from jax.sharding import PartitionSpec as P

D = 16384
HEADS = 128
KV_HEADS = 8
CHUNK_UNITS = (3, 4, 3, 3)
VMEM = 48 * 1024 * 1024


def partner(x, axis, distance):
    return lax.ppermute(x, axis, [(i, i ^ distance) for i in range(lax.axis_size(axis))])


def along_line(x, step):
    chips = lax.axis_size("blk") // 2
    hops = [(step - 1, step), (chips - step, chips - step - 1)]
    return lax.ppermute(x, "blk", [(2 * a + c, 2 * b + c) for a, b in hops for c in range(2)])


def gate_up_kernel(n_blocks, ride_at, place_ref, *refs):
    blocks, gate_ref, up_ref = refs[:n_blocks], refs[n_blocks], refs[n_blocks + 1]
    *_, first_ref, second_ref, send_ref, x_ref = refs if ride_at is None else refs[:-2] + refs[-1:]
    if ride_at is not None:
        refs[-2][...] = refs[ride_at][...]
    rows = blocks[0].shape[0]
    quarter = first_ref.shape[1]

    @pl.when(pl.program_id(0) == 0)
    def _():
        for i, block in enumerate(blocks):
            x_ref[pl.ds(pl.multiple_of(place_ref[i] * rows, rows), rows), :] = block[...]

    for i, weight in enumerate((gate_ref, up_ref)):
        y = jnp.dot(x_ref[...], weight[...], preferred_element_type=jnp.float32)
        first_ref[i] = y[:quarter]
        second_ref[i] = y[quarter : 2 * quarter]
        send_ref[i] = y[2 * quarter :].astype(jnp.bfloat16)


def gate_up(place, blocks, gate_weight, up_weight, unit, start, units, after, ride=None):
    rows, depth = blocks[0].shape
    total = rows * len(blocks)
    quarter = total // 4
    cols = units * unit
    weight_spec = pl.BlockSpec((depth, unit), lambda i: (0, start + i))
    rides = [] if ride is None else [ride]
    ride_spec = [pl.BlockSpec(r.shape, lambda i: (0, 0)) for r in rides]
    return pl.pallas_call(
        functools.partial(gate_up_kernel, len(blocks), len(blocks) + 2 if rides else None),
        grid=(units,),
        in_specs=[pl.BlockSpec(memory_space=pltpu.SMEM)]
        + [pl.BlockSpec((rows, depth), lambda i: (0, 0))] * len(blocks)
        + [weight_spec, weight_spec]
        + ride_spec
        + [pl.BlockSpec(memory_space=pl.ANY)] * len(after),
        out_specs=[
            pl.BlockSpec((2, quarter, unit), lambda i: (0, 0, i)),
            pl.BlockSpec((2, quarter, unit), lambda i: (0, 0, i)),
            pl.BlockSpec((2, 2 * quarter, unit), lambda i: (0, 0, i)),
        ]
        + ride_spec,
        out_shape=[
            jax.ShapeDtypeStruct((2, quarter, cols), jnp.float32),
            jax.ShapeDtypeStruct((2, quarter, cols), jnp.float32),
            jax.ShapeDtypeStruct((2, 2 * quarter, cols), jnp.bfloat16),
        ]
        + [jax.ShapeDtypeStruct(r.shape, r.dtype) for r in rides],
        scratch_shapes=[pltpu.VMEM((total, depth), jnp.bfloat16)],
        compiler_params=pltpu.CompilerParams(vmem_limit_bytes=VMEM),
        cost_estimate=pl.CostEstimate(
            flops=4 * total * depth * cols,
            bytes_accessed=4 * depth * cols + 2 * total * depth + 12 * total * cols,
            transcendentals=0,
        ),
    )(place, *blocks, gate_weight, up_weight, *rides, *after)


def hidden_kernel(flow_ref, own_ref, other_ref, inverse_ref, out_ref):
    inverse = inverse_ref[...]
    gate, up = [
        (own_ref[i] + other_ref[i].astype(jnp.float32) + flow_ref[i].astype(jnp.float32)) * inverse
        for i in range(2)
    ]
    out_ref[...] = (gate / (1 + jnp.exp(-gate)) * up).astype(out_ref.dtype)


def hidden_units(flow, own, other, inverse):
    _, rows, cols = own.shape
    tile = 256
    return pl.pallas_call(
        hidden_kernel,
        grid=(cols // tile,),
        in_specs=[
            pl.BlockSpec((2, rows, tile), lambda i: (0, 0, i)),
            pl.BlockSpec((2, rows, tile), lambda i: (0, 0, i)),
            pl.BlockSpec((2, rows, tile), lambda i: (0, 1, i)),
            pl.BlockSpec((rows, 1), lambda i: (0, 0)),
        ],
        out_specs=pl.BlockSpec((rows, tile), lambda i: (0, i)),
        out_shape=jax.ShapeDtypeStruct((rows, cols), jnp.bfloat16),
        cost_estimate=pl.CostEstimate(
            flops=16 * rows * cols, bytes_accessed=18 * rows * cols, transcendentals=rows * cols
        ),
    )(flow, own, other, inverse)


def down_kernel(has_total, *refs):
    parts, weight_ref, total_ref, out_ref = refs[:4], refs[4], refs[5], refs[-1]
    x = jnp.concatenate([part[...] for part in parts], axis=0)
    y = jnp.dot(x, weight_ref[...], preferred_element_type=jnp.float32)

    @pl.when(pl.program_id(0) == 0)
    def _():
        if has_total:
            out_ref[...] = total_ref[...] + y
        else:
            out_ref[...] = y

    @pl.when(pl.program_id(0) > 0)
    def _():
        out_ref[...] += y


def down(parts, weight, total, unit, start, units, after):
    quarter = parts[0].shape[0]
    width = weight.shape[1]
    out = pl.BlockSpec((4 * quarter, width), lambda i: (0, 0))
    has_total = total is not None
    return pl.pallas_call(
        functools.partial(down_kernel, has_total),
        grid=(units,),
        in_specs=[pl.BlockSpec((quarter, unit), lambda i: (0, i))] * 4
        + [pl.BlockSpec((unit, width), lambda i: (start + i, 0))]
        + [out] * has_total
        + [pl.BlockSpec(memory_space=pl.ANY)] * len(after),
        out_specs=out,
        out_shape=jax.ShapeDtypeStruct((4 * quarter, width), jnp.float32),
        input_output_aliases={5: 0} if has_total else {},
        compiler_params=pltpu.CompilerParams(vmem_limit_bytes=VMEM),
        cost_estimate=pl.CostEstimate(
            flops=8 * quarter * units * unit * width,
            bytes_accessed=2 * units * unit * width + 32 * quarter * width,
            transcendentals=0,
        ),
    )(*parts, weight, *([total] if has_total else []), *after)


def attend(residual_in, queries, key_cache, value_cache, key_new, value_new, lengths):
    cycle_size = lax.axis_size("blk")
    quarters = cycle_size // KV_HEADS
    per_kv = HEADS // KV_HEADS
    own_heads = HEADS // cycle_size
    head_size = key_cache.shape[3]
    seq_rows = residual_in.shape[0]
    positions_here = key_cache.shape[2]
    blk_index = lax.axis_index("blk")
    kv_head = blk_index // quarters
    quarter = blk_index % quarters
    score_scale = 1.0 / math.sqrt(head_size)
    group_queries = lax.dynamic_slice_in_dim(
        queries, kv_head * per_kv * head_size, per_kv * head_size, 1
    )
    group_queries = group_queries.astype(jnp.float32).reshape(seq_rows, per_kv, head_size)
    fresh_key = lax.dynamic_slice_in_dim(key_new, kv_head * head_size, head_size, 1).astype(
        jnp.float32
    )
    fresh_value = lax.dynamic_slice_in_dim(value_new, kv_head * head_size, head_size, 1).astype(
        jnp.float32
    )
    keys_here = key_cache[:, 0].astype(jnp.float32)
    values_here = value_cache[:, 0].astype(jnp.float32)
    scores = jnp.einsum("shd,spd->shp", group_queries, keys_here) * score_scale
    fresh_scores = jnp.einsum("shd,sd->sh", group_queries, fresh_key) * score_scale
    places = quarter * positions_here + jnp.arange(positions_here, dtype=jnp.int32)
    usable = (places[None, :] < lengths[:, None])[:, None, :]
    with_fresh = quarter == 0
    largest = jnp.maximum(
        jnp.max(jnp.where(usable, scores, -1e30), axis=2),
        jnp.where(with_fresh, fresh_scores, -1e30),
    )
    weights = jnp.where(usable, jnp.exp(scores - largest[..., None]), 0.0)
    fresh_weight = jnp.where(with_fresh, jnp.exp(fresh_scores - largest), 0.0)
    totals = jnp.sum(weights, axis=2) + fresh_weight
    weighted = (
        jnp.einsum("shp,spd->shd", weights, values_here)
        + fresh_weight[..., None] * fresh_value[:, None, :]
    )
    for bit_number in range(quarters.bit_length() - 1):
        peer_max, peer_total, peer_weighted = partner(
            (largest, totals, weighted), "blk", 1 << bit_number
        )
        merged = jnp.maximum(largest, peer_max)
        mine_factor = jnp.exp(largest - merged)
        peer_factor = jnp.exp(peer_max - merged)
        totals = totals * mine_factor + peer_total * peer_factor
        weighted = weighted * mine_factor[..., None] + peer_weighted * peer_factor[..., None]
        largest = merged
    attention = weighted / totals[..., None]
    own_output = lax.dynamic_slice_in_dim(attention, quarter * own_heads, own_heads, 1).reshape(
        seq_rows, own_heads * head_size
    )
    return residual_in.astype(jnp.float32) + own_output


def on_device(
    residual_in,
    queries,
    key_cache,
    value_cache,
    key_new,
    value_new,
    lengths,
    ffn_gain,
    gate_weight,
    up_weight,
    down_weight,
):
    groups = lax.axis_size("grp")
    group = lax.axis_index("grp")
    chips = lax.axis_size("blk") // 2
    chip, core = lax.axis_index("blk") // 2, lax.axis_index("blk") % 2
    rows = residual_in.shape[0]
    per_quarter = groups // 4
    quarter = per_quarter * rows

    wide = attend(residual_in, queries, key_cache, value_cache, key_new, value_new, lengths)

    tokens = (wide * ffn_gain.astype(jnp.float32)[None, :]).astype(jnp.bfloat16)
    blocks = [tokens] + [partner(tokens, "grp", i) for i in range(1, groups)]

    squares = jnp.sum(wide * wide, axis=1)
    for bit_number in range(lax.axis_size("blk").bit_length() - 1):
        squares = squares + partner(squares, "blk", 1 << bit_number)

    lead = 2 * core + jnp.where(chip >= chips // 2, 0, 1)
    turn = group ^ (lead * per_quarter)
    place = jnp.arange(groups, dtype=jnp.int32) ^ turn
    last_rows = jnp.arange(per_quarter, dtype=jnp.int32) + per_quarter
    unit = gate_weight.shape[1] // sum(CHUNK_UNITS)
    edges = [sum(CHUNK_UNITS[:i]) for i in range(len(CHUNK_UNITS) + 1)]
    f32 = jnp.float32
    passed, chunks = [], []
    inverse = None
    for k, units in enumerate(CHUNK_UNITS):
        after = [passed[k - 2 - i][i] for i in range(min(k - 1, chips - 1))]
        ride = squares[None, :] if k == 0 else None
        first, second, send, *rides = gate_up(
            place, blocks, gate_weight, up_weight, unit, edges[k], units, after, ride
        )
        if k == 0:
            squares = rides[0][0]
            squares = [squares] + [partner(squares, "grp", i) for i in range(1, groups)]
            squares = jnp.stack(squares)[last_rows ^ turn].reshape(quarter, 1)
            inverse = lax.rsqrt(squares / D + 1e-05)
        other = partner(send, "blk", 1)
        with_other = [first + other[:, :quarter].astype(f32), second + other[:, quarter:].astype(f32)]
        flow = None
        passed.append([])
        for step in range(1, chips):
            own = with_other[step > chips // 2]
            flow = (own if flow is None else own + flow.astype(f32)).astype(jnp.bfloat16)
            passed[k].append(flow)
            flow = along_line(flow, step)
        hidden = hidden_units(flow, second, other, inverse)
        halves = [hidden, None]
        for step in range(1, chips):
            passed[k].append(hidden)
            hidden = along_line(hidden, step)
            half = step // (chips // 2)
            here = (chip == step) | (chip == chips - 1 - step)
            halves[half] = hidden if halves[half] is None else jnp.where(here, hidden, halves[half])
        halves = [halves[1], halves[0]]
        chunks.append(halves + [partner(half, "blk", 1) for half in halves])
    total = None
    for k, units in enumerate(CHUNK_UNITS):
        after = [passed[k + 1 + i][-i] for i in range(1, chips - 1) if k + 1 + i < len(passed)]
        total = down(chunks[k], down_weight, total, unit, edges[k], units, after)

    terms = total.reshape(groups, rows, -1)
    own = lax.dynamic_index_in_dim(terms, turn, 0, keepdims=False)
    out = wide + own
    for i in range(1, groups):
        term = lax.dynamic_index_in_dim(terms, turn ^ i, 0, keepdims=False)
        out = out + partner(term.astype(jnp.bfloat16), "grp", i).astype(f32)
    return out


def solution(mesh):
    in_specs = (
        P("grp", "blk"),
        P("grp", None),
        P("grp", "blk", None, None),
        P("grp", "blk", None, None),
        P("grp", None),
        P("grp", None),
        P("grp"),
        P("blk"),
        P("blk", "grp"),
        P("blk", "grp"),
        P("grp", "blk"),
    )
    out_specs = P("grp", "blk")
    return jax.shard_map(
        on_device, mesh=mesh, in_specs=in_specs, out_specs=out_specs, check_vma=False
    )
```

```python
import functools
import math

import jax
import jax.numpy as jnp
from jax import lax
from jax.experimental import pallas as pl
from jax.experimental.pallas import tpu as pltpu
from jax.sharding import PartitionSpec as P

D = 16384
HEADS = 128
KV_HEADS = 8
CHUNK_UNITS = (4, 6, 6, 6, 4)
SLOTS = 4
VMEM = 40 * 1024 * 1024
SMALL_VMEM = 8 * 1024 * 1024


def partner(x, axis, distance):
    return lax.ppermute(x, axis, [(i, i ^ distance) for i in range(lax.axis_size(axis))])


def along_line(x, step):
    chips = lax.axis_size("blk") // 2
    hops = [(step - 1, step), (chips - step, chips - step - 1)]
    return lax.ppermute(x, "blk", [(2 * a + c, 2 * b + c) for a, b in hops for c in range(2)])


def stream(units, copies, compute):
    def start(i, slot):
        for copy in copies(i, slot):
            copy.start()

    for i in range(min(SLOTS - 1, units)):
        start(i, i)

    def step(i, _):
        later = i + SLOTS - 1

        @pl.when(later < units)
        def _():
            start(later, lax.rem(later, SLOTS))

        slot = lax.rem(i, SLOTS)
        for copy in copies(i, slot):
            copy.wait()
        compute(i, slot)
        return 0

    lax.fori_loop(0, units, step, 0)


def gate_up_kernel(n_blocks, has_ride, first_unit, units, place_ref, *refs):
    blocks, gate_ref, up_ref = refs[:n_blocks], refs[n_blocks], refs[n_blocks + 1]
    first_ref, second_ref, send_ref, *rest = refs[-6 - has_ride :]
    x_ref, held, sems = rest[-3:]
    if has_ride:
        rest[0][...] = refs[n_blocks + 2][...]
    rows = blocks[0].shape[0]
    quarter = first_ref.shape[1]
    unit = held.shape[3]

    def copies(i, slot):
        columns = pl.ds(pl.multiple_of((first_unit + i) * unit, unit), unit)
        return [
            pltpu.make_async_copy(weight.at[:, columns], held.at[slot, j], sems.at[slot, j])
            for j, weight in enumerate((gate_ref, up_ref))
        ]

    def compute(i, slot):
        columns = pl.ds(pl.multiple_of(i * unit, unit), unit)

        @pl.when(i == 0)
        def _():
            for j, block in enumerate(blocks):
                x_ref[pl.ds(pl.multiple_of(place_ref[j] * rows, rows), rows), :] = block[...]

        for j in range(2):
            y = jnp.dot(x_ref[...], held[slot, j], preferred_element_type=jnp.float32)
            first_ref[j, :, columns] = y[:quarter]
            second_ref[j, :, columns] = y[quarter : 2 * quarter]
            send_ref[j, :, columns] = y[2 * quarter :].astype(jnp.bfloat16)

    stream(units, copies, compute)


def gate_up(place, blocks, gate_weight, up_weight, unit, start, units, after, ride=None):
    rows, depth = blocks[0].shape
    total = rows * len(blocks)
    quarter = total // 4
    cols = units * unit
    rides = [] if ride is None else [ride]
    vmem = pl.BlockSpec(memory_space=pltpu.VMEM)
    anywhere = pl.BlockSpec(memory_space=pl.ANY)
    return pl.pallas_call(
        functools.partial(gate_up_kernel, len(blocks), len(rides), start, units),
        in_specs=[pl.BlockSpec(memory_space=pltpu.SMEM)]
        + [vmem] * len(blocks)
        + [pl.BlockSpec(memory_space=pltpu.HBM)] * 2
        + [vmem] * len(rides)
        + [anywhere] * len(after),
        out_specs=[vmem] * (3 + len(rides)),
        out_shape=[
            jax.ShapeDtypeStruct((2, quarter, cols), jnp.float32),
            jax.ShapeDtypeStruct((2, quarter, cols), jnp.float32),
            jax.ShapeDtypeStruct((2, 2 * quarter, cols), jnp.bfloat16),
        ]
        + [jax.ShapeDtypeStruct(r.shape, r.dtype) for r in rides],
        scratch_shapes=[
            pltpu.VMEM((total, depth), jnp.bfloat16),
            pltpu.VMEM((SLOTS, 2, depth, unit), jnp.bfloat16),
            pltpu.SemaphoreType.DMA((SLOTS, 2)),
        ],
        compiler_params=pltpu.CompilerParams(vmem_limit_bytes=VMEM),
        cost_estimate=pl.CostEstimate(
            flops=4 * total * depth * cols,
            bytes_accessed=4 * depth * cols + 2 * total * depth + 12 * total * cols,
            transcendentals=0,
        ),
    )(place, *blocks, gate_weight, up_weight, *rides, *after)


def pass_on_kernel(half, has_flow, own_ref, other_ref, *refs):
    rows = own_ref.shape[1]
    total = own_ref[...] + other_ref[:, half * rows : (half + 1) * rows].astype(jnp.float32)
    if has_flow:
        total = total + refs[0][...].astype(jnp.float32)
    refs[-1][...] = total.astype(jnp.bfloat16)


def pass_on(half, own, other, flow, after):
    vmem = pl.BlockSpec(memory_space=pltpu.VMEM)
    flows = [] if flow is None else [flow]
    return pl.pallas_call(
        functools.partial(pass_on_kernel, half, len(flows)),
        in_specs=[vmem] * (2 + len(flows)) + [pl.BlockSpec(memory_space=pl.ANY)] * len(after),
        out_specs=vmem,
        out_shape=jax.ShapeDtypeStruct(own.shape, jnp.bfloat16),
        compiler_params=pltpu.CompilerParams(vmem_limit_bytes=SMALL_VMEM),
        cost_estimate=pl.CostEstimate(
            flops=2 * own.size, bytes_accessed=10 * own.size, transcendentals=0
        ),
    )(own, other, *flows, *after)


def hidden_kernel(flow_ref, own_ref, other_ref, inverse_ref, *refs):
    rows = own_ref.shape[1]
    inverse = inverse_ref[...]
    gate, up = [
        (
            own_ref[i]
            + other_ref[i, rows:].astype(jnp.float32)
            + flow_ref[i].astype(jnp.float32)
        )
        * inverse
        for i in range(2)
    ]
    refs[-1][...] = (gate / (1 + jnp.exp(-gate)) * up).astype(jnp.bfloat16)


def hidden_units(flow, own, other, inverse, after):
    _, rows, cols = own.shape
    vmem = pl.BlockSpec(memory_space=pltpu.VMEM)
    return pl.pallas_call(
        hidden_kernel,
        in_specs=[vmem] * 4 + [pl.BlockSpec(memory_space=pl.ANY)] * len(after),
        out_specs=vmem,
        out_shape=jax.ShapeDtypeStruct((rows, cols), jnp.bfloat16),
        compiler_params=pltpu.CompilerParams(vmem_limit_bytes=SMALL_VMEM),
        cost_estimate=pl.CostEstimate(
            flops=16 * rows * cols, bytes_accessed=18 * rows * cols, transcendentals=rows * cols
        ),
    )(flow, own, other, inverse, *after)


def halves_kernel(n_stages, near_ref, *refs):
    stages, out_ref = refs[:n_stages], refs[-1]
    for i, stage in enumerate(stages):
        half = 1 if i < len(stages) // 2 else 0

        @pl.when((near_ref[0] == i) | (near_ref[0] == len(stages) - 1 - i))
        def _():
            out_ref[half] = stage[...]


def both_halves(near, stages, after):
    vmem = pl.BlockSpec(memory_space=pltpu.VMEM)
    return pl.pallas_call(
        functools.partial(halves_kernel, len(stages)),
        in_specs=[pl.BlockSpec(memory_space=pltpu.SMEM)]
        + [vmem] * len(stages)
        + [pl.BlockSpec(memory_space=pl.ANY)] * len(after),
        out_specs=vmem,
        out_shape=jax.ShapeDtypeStruct((2, *stages[0].shape), stages[0].dtype),
        compiler_params=pltpu.CompilerParams(vmem_limit_bytes=SMALL_VMEM),
        cost_estimate=pl.CostEstimate(
            flops=0, bytes_accessed=8 * stages[0].size, transcendentals=0
        ),
    )(near, *stages, *after)


def down_kernel(has_total, n_outs, first_unit, units, place_ref, *refs):
    ours_ref, theirs_ref, weight_ref = refs[:3]
    is_last = n_outs > 1
    x_ref, held, sems, *rest = refs[len(refs) - 3 - is_last :]
    outs = refs[len(refs) - 3 - is_last - n_outs : len(refs) - 3 - is_last]
    total_ref = rest[0] if is_last else outs[0]
    quarter = ours_ref.shape[1]
    unit = held.shape[1]

    def copies(i, slot):
        here = pl.ds(pl.multiple_of((first_unit + i) * unit, unit), unit)
        return [pltpu.make_async_copy(weight_ref.at[here, :], held.at[slot], sems.at[slot])]

    def compute(i, slot):
        @pl.when(i == 0)
        def _():
            for j in range(4):
                part = (ours_ref, theirs_ref)[j // 2]
                x_ref[quarter * j : quarter * (j + 1), :] = part[j % 2]
            total_ref[...] = refs[3][...] if has_total else jnp.zeros_like(total_ref)

        x = x_ref[:, pl.ds(pl.multiple_of(i * unit, unit), unit)]
        total_ref[...] += jnp.dot(x, held[slot], preferred_element_type=jnp.float32)

    stream(units, copies, compute)
    if is_last:
        for j, out_ref in enumerate(outs):
            rows = out_ref.shape[0]
            term = total_ref[pl.ds(pl.multiple_of(place_ref[j] * rows, rows), rows), :]
            out_ref[...] = term.astype(out_ref.dtype)
    else:
        outs[0][...] = total_ref[...]


def down(place, ours, theirs, weight, total, unit, start, units, after, is_last):
    groups = place.shape[0]
    quarter, cols = ours.shape[1:]
    width = weight.shape[1]
    has_total = total is not None
    vmem = pl.BlockSpec(memory_space=pltpu.VMEM)
    anywhere = pl.BlockSpec(memory_space=pl.ANY)
    rows = 4 * quarter // groups
    outs = [jax.ShapeDtypeStruct((4 * quarter, width), jnp.float32)]
    if is_last:
        outs = [jax.ShapeDtypeStruct((rows, width), jnp.float32)]
        outs += [jax.ShapeDtypeStruct((rows, width), jnp.bfloat16)] * (groups - 1)
    return pl.pallas_call(
        functools.partial(down_kernel, has_total, len(outs), start, units),
        in_specs=[pl.BlockSpec(memory_space=pltpu.SMEM), vmem, vmem]
        + [pl.BlockSpec(memory_space=pltpu.HBM)]
        + [vmem] * has_total
        + [anywhere] * len(after),
        out_specs=[vmem] * len(outs),
        out_shape=outs,
        scratch_shapes=[
            pltpu.VMEM((4 * quarter, cols), jnp.bfloat16),
            pltpu.VMEM((SLOTS, unit, width), jnp.bfloat16),
            pltpu.SemaphoreType.DMA((SLOTS,)),
        ]
        + [pltpu.VMEM((4 * quarter, width), jnp.float32)] * is_last,
        compiler_params=pltpu.CompilerParams(vmem_limit_bytes=VMEM),
        cost_estimate=pl.CostEstimate(
            flops=8 * quarter * units * unit * width,
            bytes_accessed=2 * units * unit * width + 32 * quarter * width,
            transcendentals=0,
        ),
    )(place, ours, theirs, weight, *([total] if has_total else []), *after)


def attend(residual_in, queries, key_cache, value_cache, key_new, value_new, lengths):
    cycle_size = lax.axis_size("blk")
    quarters = cycle_size // KV_HEADS
    per_kv = HEADS // KV_HEADS
    own_heads = HEADS // cycle_size
    head_size = key_cache.shape[3]
    seq_rows = residual_in.shape[0]
    positions_here = key_cache.shape[2]
    blk_index = lax.axis_index("blk")
    kv_head = blk_index // quarters
    quarter = blk_index % quarters
    score_scale = 1.0 / math.sqrt(head_size)
    group_queries = lax.dynamic_slice_in_dim(
        queries, kv_head * per_kv * head_size, per_kv * head_size, 1
    )
    group_queries = group_queries.astype(jnp.float32).reshape(seq_rows, per_kv, head_size)
    fresh_key = lax.dynamic_slice_in_dim(key_new, kv_head * head_size, head_size, 1).astype(
        jnp.float32
    )
    fresh_value = lax.dynamic_slice_in_dim(value_new, kv_head * head_size, head_size, 1).astype(
        jnp.float32
    )
    keys_here = key_cache[:, 0].astype(jnp.float32)
    values_here = value_cache[:, 0].astype(jnp.float32)
    scores = jnp.einsum("shd,spd->shp", group_queries, keys_here) * score_scale
    fresh_scores = jnp.einsum("shd,sd->sh", group_queries, fresh_key) * score_scale
    places = quarter * positions_here + jnp.arange(positions_here, dtype=jnp.int32)
    usable = (places[None, :] < lengths[:, None])[:, None, :]
    with_fresh = quarter == 0
    largest = jnp.maximum(
        jnp.max(jnp.where(usable, scores, -1e30), axis=2),
        jnp.where(with_fresh, fresh_scores, -1e30),
    )
    weights = jnp.where(usable, jnp.exp(scores - largest[..., None]), 0.0)
    fresh_weight = jnp.where(with_fresh, jnp.exp(fresh_scores - largest), 0.0)
    totals = jnp.sum(weights, axis=2) + fresh_weight
    weighted = (
        jnp.einsum("shp,spd->shd", weights, values_here)
        + fresh_weight[..., None] * fresh_value[:, None, :]
    )
    for bit_number in range(quarters.bit_length() - 1):
        peer_max, peer_total, peer_weighted = partner(
            (largest, totals, weighted), "blk", 1 << bit_number
        )
        merged = jnp.maximum(largest, peer_max)
        mine_factor = jnp.exp(largest - merged)
        peer_factor = jnp.exp(peer_max - merged)
        totals = totals * mine_factor + peer_total * peer_factor
        weighted = weighted * mine_factor[..., None] + peer_weighted * peer_factor[..., None]
        largest = merged
    attention = weighted / totals[..., None]
    own_output = lax.dynamic_slice_in_dim(attention, quarter * own_heads, own_heads, 1).reshape(
        seq_rows, own_heads * head_size
    )
    return residual_in.astype(jnp.float32) + own_output


def on_device(
    residual_in,
    queries,
    key_cache,
    value_cache,
    key_new,
    value_new,
    lengths,
    ffn_gain,
    gate_weight,
    up_weight,
    down_weight,
):
    groups = lax.axis_size("grp")
    group = lax.axis_index("grp")
    chips = lax.axis_size("blk") // 2
    chip, core = lax.axis_index("blk") // 2, lax.axis_index("blk") % 2
    rows = residual_in.shape[0]
    per_quarter = groups // 4
    quarter = per_quarter * rows

    wide = attend(residual_in, queries, key_cache, value_cache, key_new, value_new, lengths)

    tokens = (wide * ffn_gain.astype(jnp.float32)[None, :]).astype(jnp.bfloat16)
    blocks = [tokens] + [partner(tokens, "grp", i) for i in range(1, groups)]

    squares = jnp.sum(wide * wide, axis=1)
    for bit_number in range(lax.axis_size("blk").bit_length() - 1):
        squares = squares + partner(squares, "blk", 1 << bit_number)

    lead = 2 * core + jnp.where(chip >= chips // 2, 0, 1)
    turn = group ^ (lead * per_quarter)
    place = jnp.arange(groups, dtype=jnp.int32) ^ turn
    last_rows = jnp.arange(per_quarter, dtype=jnp.int32) + per_quarter
    unit = gate_weight.shape[1] // sum(CHUNK_UNITS)
    edges = [sum(CHUNK_UNITS[:i]) for i in range(len(CHUNK_UNITS) + 1)]
    f32 = jnp.float32
    n_chunks = len(CHUNK_UNITS)
    near = jnp.minimum(chip, chips - 1 - chip).reshape(1)
    inverse, total = None, None
    chunks = [{} for _ in range(n_chunks)]
    last = []

    order = [0, 2 * chips, 2 * chips - 1, *range(chips, 0, -1)]
    for turn_number in range(n_chunks + 2 * chips):
        for stage in order:
            k = turn_number - stage
            if stage == 2 * chips - 1:
                for j in range(1, chips - 1):
                    if 0 <= turn_number - chips - j < n_chunks:
                        last = last + [chunks[turn_number - chips - j]["stages"][j]]
                if turn_number == 1:
                    last = last + squares
                    squares = jnp.stack(squares)[last_rows ^ turn].reshape(quarter, 1)
                    inverse = lax.rsqrt(squares / D + 1e-05)
            if not 0 <= k < n_chunks:
                continue
            units, chunk = CHUNK_UNITS[k], chunks[k]
            if stage == 0:
                ride = squares[None, :] if k == 0 else None
                first, second, send, *rides = gate_up(
                    place, blocks, gate_weight, up_weight, unit, edges[k], units, last, ride
                )
                last = [send]
                chunk.update(own=(first, second), flow=None, other=partner(send, "blk", 1))
                if k == 0:
                    squares = rides[0][0]
                    squares = [squares] + [partner(squares, "grp", i) for i in range(1, groups)]
            elif stage < chips:
                half = int(stage > chips // 2)
                flow = pass_on(half, chunk["own"][half], chunk["other"], chunk["flow"], last)
                last = [flow]
                chunk["flow"] = along_line(flow, stage)
            elif stage == chips:
                hidden = hidden_units(
                    chunk["flow"], chunk["own"][1], chunk["other"], inverse, last
                )
                last = [hidden]
                stages = [hidden]
                for step in range(1, chips):
                    stages.append(along_line(stages[-1], step))
                chunk["stages"] = stages
            elif stage == 2 * chips - 1:
                ours = both_halves(near, chunk["stages"], last)
                last = [ours]
                chunk.update(ours=ours, theirs=partner(ours, "blk", 1))
            else:
                total, *send = down(
                    place,
                    chunk["ours"],
                    chunk["theirs"],
                    down_weight,
                    total,
                    2 * unit,
                    edges[k] // 2,
                    units // 2,
                    last,
                    k == n_chunks - 1,
                )
                last = [total]

    out = wide + total
    for i in range(1, groups):
        out = out + partner(send[i - 1], "grp", i).astype(f32)
    return out


def solution(mesh):
    in_specs = (
        P("grp", "blk"),
        P("grp", None),
        P("grp", "blk", None, None),
        P("grp", "blk", None, None),
        P("grp", None),
        P("grp", None),
        P("grp"),
        P("blk"),
        P("blk", "grp"),
        P("blk", "grp"),
        P("grp", "blk"),
    )
    out_specs = P("grp", "blk")
    return jax.shard_map(
        on_device, mesh=mesh, in_specs=in_specs, out_specs=out_specs, check_vma=False
    )
```

```python
import functools
import math

import jax
import jax.numpy as jnp
from jax import lax
from jax.experimental import pallas as pl
from jax.experimental.pallas import tpu as pltpu
from jax.sharding import PartitionSpec as P

D = 16384
HEADS = 128
KV_HEADS = 8
CHUNK_UNITS = (8, 10, 8)
SLOTS = 3
VMEM = 38 * 1024 * 1024
SMALL_VMEM = 8 * 1024 * 1024


def partner(x, axis, distance):
    return lax.ppermute(x, axis, [(i, i ^ distance) for i in range(lax.axis_size(axis))])


def along_ring(x):
    chips = lax.axis_size("blk") // 2
    ring = [0, *range(1, chips, 2), *range(chips - 2, 0, -2)]
    hops = zip(ring, ring[1:] + ring[:1])
    return lax.ppermute(x, "blk", [(2 * a + c, 2 * b + c) for a, b in hops for c in range(2)])


def stream(units, copies, prepare, compute):
    def start(i, slot):
        for copy in copies(i, slot):
            copy.start()

    for i in range(min(SLOTS - 1, units)):
        start(i, i)
    prepare()

    def step(i, _):
        later = i + SLOTS - 1

        @pl.when(later < units)
        def _():
            start(later, lax.rem(later, SLOTS))

        slot = lax.rem(i, SLOTS)
        for copy in copies(i, slot):
            copy.wait()
        compute(i, slot)
        return 0

    lax.fori_loop(0, units, step, 0)


def gate_up_kernel(n_blocks, has_ride, first_unit, units, place_ref, *refs):
    blocks, gate_ref, up_ref = refs[:n_blocks], refs[n_blocks], refs[n_blocks + 1]
    keep_ref, send_ref, *rest = refs[-5 - has_ride :]
    x_ref, held, sems = rest[-3:]
    half = keep_ref.shape[1]
    unit = held.shape[3]
    parts = place_ref.shape[0] // n_blocks
    rows = blocks[0].shape[0] // parts

    def copies(i, slot):
        columns = pl.ds(pl.multiple_of((first_unit + i) * unit, unit), unit)
        return [
            pltpu.make_async_copy(weight.at[:, columns], held.at[slot, j], sems.at[slot, j])
            for j, weight in enumerate((gate_ref, up_ref))
        ]

    def prepare():
        if has_ride:
            rest[0][...] = refs[n_blocks + 2][...]
        for i in range(n_blocks * parts):
            to = pl.ds(pl.multiple_of(place_ref[i] * rows, rows), rows)
            x_ref[to, :] = blocks[i // parts][i % parts * rows : (i % parts + 1) * rows, :]

    def compute(i, slot):
        columns = pl.ds(pl.multiple_of(i * unit, unit), unit)
        for j in range(2):
            y = jnp.dot(x_ref[...], held[slot, j], preferred_element_type=jnp.float32)
            keep_ref[j, :, columns] = y[:half].astype(jnp.bfloat16)
            send_ref[j, :, columns] = y[half:].astype(jnp.bfloat16)

    stream(units, copies, prepare, compute)


def gate_up(place, blocks, gate_weight, up_weight, unit, start, units, after, ride=None):
    rows, depth = blocks[0].shape
    total = rows * len(blocks)
    cols = units * unit
    rides = [] if ride is None else [ride]
    vmem = pl.BlockSpec(memory_space=pltpu.VMEM)
    anywhere = pl.BlockSpec(memory_space=pl.ANY)
    return pl.pallas_call(
        functools.partial(gate_up_kernel, len(blocks), len(rides), start, units),
        in_specs=[pl.BlockSpec(memory_space=pltpu.SMEM)]
        + [vmem] * len(blocks)
        + [pl.BlockSpec(memory_space=pltpu.HBM)] * 2
        + [vmem] * len(rides)
        + [anywhere] * len(after),
        out_specs=[vmem] * (2 + len(rides)),
        out_shape=[jax.ShapeDtypeStruct((2, total // 2, cols), jnp.bfloat16)] * 2
        + [jax.ShapeDtypeStruct(r.shape, r.dtype) for r in rides],
        scratch_shapes=[
            pltpu.VMEM((total, depth), jnp.bfloat16),
            pltpu.VMEM((SLOTS, 2, depth, unit), jnp.bfloat16),
            pltpu.SemaphoreType.DMA((SLOTS, 2)),
        ],
        compiler_params=pltpu.CompilerParams(vmem_limit_bytes=VMEM),
        cost_estimate=pl.CostEstimate(
            flops=4 * total * depth * cols,
            bytes_accessed=4 * depth * cols + 2 * total * depth + 4 * total * cols,
            transcendentals=0,
        ),
    )(place, *blocks, gate_weight, up_weight, *rides, *after)


def nothing(*refs):
    pass


def hold(x, after):
    anywhere = pl.BlockSpec(memory_space=pl.ANY)
    return pl.pallas_call(
        nothing,
        in_specs=[anywhere] * (1 + len(after)),
        out_specs=anywhere,
        out_shape=jax.ShapeDtypeStruct(x.shape, x.dtype),
        input_output_aliases={0: 0},
        cost_estimate=pl.CostEstimate(flops=0, bytes_accessed=0, transcendentals=0),
    )(x, *after)


def pass_on_kernel(shard, has_flow, own_ref, other_ref, *refs):
    out_ref = refs[-1]
    rows = out_ref.shape[1]
    here = slice(shard * rows, (shard + 1) * rows)
    total = own_ref[:, here].astype(jnp.float32) + other_ref[:, here].astype(jnp.float32)
    if has_flow:
        total = total + refs[0][...].astype(jnp.float32)
    out_ref[...] = total.astype(jnp.bfloat16)


def pass_on(shard, shards, own, other, flow, after):
    vmem = pl.BlockSpec(memory_space=pltpu.VMEM)
    flows = [] if flow is None else [flow]
    return pl.pallas_call(
        functools.partial(pass_on_kernel, shard, len(flows)),
        in_specs=[vmem] * (2 + len(flows)) + [pl.BlockSpec(memory_space=pl.ANY)] * len(after),
        out_specs=vmem,
        out_shape=jax.ShapeDtypeStruct(
            (2, own.shape[1] // shards, own.shape[2]), jnp.bfloat16
        ),
        compiler_params=pltpu.CompilerParams(vmem_limit_bytes=SMALL_VMEM),
        cost_estimate=pl.CostEstimate(
            flops=2 * own.size // shards, bytes_accessed=8 * own.size // shards, transcendentals=0
        ),
    )(own, other, *flows, *after)


def hidden_kernel(flow_ref, own_ref, other_ref, inverse_ref, *refs):
    rows = flow_ref.shape[1]
    inverse = inverse_ref[...]
    gate, up = [
        (
            own_ref[i, -rows:].astype(jnp.float32)
            + other_ref[i, -rows:].astype(jnp.float32)
            + flow_ref[i].astype(jnp.float32)
        )
        * inverse
        for i in range(2)
    ]
    refs[-1][...] = (gate / (1 + jnp.exp(-gate)) * up).astype(jnp.bfloat16)


def hidden_units(flow, own, other, inverse, after):
    _, rows, cols = flow.shape
    vmem = pl.BlockSpec(memory_space=pltpu.VMEM)
    return pl.pallas_call(
        hidden_kernel,
        in_specs=[vmem] * 4 + [pl.BlockSpec(memory_space=pl.ANY)] * len(after),
        out_specs=vmem,
        out_shape=jax.ShapeDtypeStruct((rows, cols), jnp.bfloat16),
        compiler_params=pltpu.CompilerParams(vmem_limit_bytes=SMALL_VMEM),
        cost_estimate=pl.CostEstimate(
            flops=16 * rows * cols, bytes_accessed=14 * rows * cols, transcendentals=rows * cols
        ),
    )(flow, own, other, inverse, *after)


def join_kernel(n_shards, *refs):
    out_ref = refs[-1]
    rows = refs[0].shape[0]
    for i, shard in enumerate(refs[:n_shards]):
        out_ref[i * rows : (i + 1) * rows] = shard[...]


def join(shards, after):
    rows, cols = shards[0].shape
    vmem = pl.BlockSpec(memory_space=pltpu.VMEM)
    return pl.pallas_call(
        functools.partial(join_kernel, len(shards)),
        in_specs=[vmem] * len(shards) + [pl.BlockSpec(memory_space=pl.ANY)] * len(after),
        out_specs=vmem,
        out_shape=jax.ShapeDtypeStruct((rows * len(shards), cols), jnp.bfloat16),
        compiler_params=pltpu.CompilerParams(vmem_limit_bytes=SMALL_VMEM),
        cost_estimate=pl.CostEstimate(
            flops=0, bytes_accessed=4 * rows * len(shards) * cols, transcendentals=0
        ),
    )(*shards, *after)


def down_kernel(has_total, n_outs, first_unit, units, place_ref, *refs):
    ours_ref, theirs_ref, weight_ref = refs[:3]
    is_last = n_outs > 1
    x_ref, held, sems, *rest = refs[len(refs) - 3 - is_last :]
    outs = refs[len(refs) - 3 - is_last - n_outs : len(refs) - 3 - is_last]
    total_ref = rest[0] if is_last else outs[0]
    half = ours_ref.shape[0]
    unit = held.shape[1]

    def copies(i, slot):
        here = pl.ds(pl.multiple_of((first_unit + i) * unit, unit), unit)
        return [pltpu.make_async_copy(weight_ref.at[here, :], held.at[slot], sems.at[slot])]

    def prepare():
        x_ref[:half] = ours_ref[...]
        x_ref[half:] = theirs_ref[...]
        total_ref[...] = refs[3][...] if has_total else jnp.zeros_like(total_ref)

    def compute(i, slot):
        x = x_ref[:, pl.ds(pl.multiple_of(i * unit, unit), unit)]
        total_ref[...] += jnp.dot(x, held[slot], preferred_element_type=jnp.float32)

    stream(units, copies, prepare, compute)
    if is_last:
        parts = place_ref.shape[0] // n_outs
        for i in range(n_outs * parts):
            out_ref = outs[i // parts]
            rows = out_ref.shape[0] // parts
            term = total_ref[pl.ds(pl.multiple_of(place_ref[i] * rows, rows), rows), :]
            out_ref[i % parts * rows : (i % parts + 1) * rows, :] = term.astype(out_ref.dtype)


def down(place, groups, ours, theirs, weight, total, unit, start, units, after, is_last):
    half, cols = ours.shape
    width = weight.shape[1]
    has_total = total is not None
    vmem = pl.BlockSpec(memory_space=pltpu.VMEM)
    rows = 2 * half // groups
    outs = [jax.ShapeDtypeStruct((2 * half, width), jnp.float32)]
    if is_last:
        outs = [jax.ShapeDtypeStruct((rows, width), jnp.float32)]
        outs += [jax.ShapeDtypeStruct((rows, width), jnp.bfloat16)] * (groups - 1)
    return pl.pallas_call(
        functools.partial(down_kernel, has_total, len(outs), start, units),
        in_specs=[pl.BlockSpec(memory_space=pltpu.SMEM), vmem, vmem]
        + [pl.BlockSpec(memory_space=pltpu.HBM)]
        + [vmem] * has_total
        + [pl.BlockSpec(memory_space=pl.ANY)] * len(after),
        out_specs=[vmem] * len(outs),
        out_shape=outs,
        scratch_shapes=[
            pltpu.VMEM((2 * half, cols), jnp.bfloat16),
            pltpu.VMEM((SLOTS, unit, width), jnp.bfloat16),
            pltpu.SemaphoreType.DMA((SLOTS,)),
        ]
        + [pltpu.VMEM((2 * half, width), jnp.float32)] * is_last,
        compiler_params=pltpu.CompilerParams(vmem_limit_bytes=VMEM),
        cost_estimate=pl.CostEstimate(
            flops=4 * half * units * unit * width,
            bytes_accessed=2 * units * unit * width + 16 * half * width,
            transcendentals=0,
        ),
    )(place, ours, theirs, weight, *([total] if has_total else []), *after)


def attend(residual_in, queries, key_cache, value_cache, key_new, value_new, lengths):
    cycle_size = lax.axis_size("blk")
    quarters = cycle_size // KV_HEADS
    per_kv = HEADS // KV_HEADS
    own_heads = HEADS // cycle_size
    head_size = key_cache.shape[3]
    seq_rows = residual_in.shape[0]
    positions_here = key_cache.shape[2]
    blk_index = lax.axis_index("blk")
    kv_head = blk_index // quarters
    quarter = blk_index % quarters
    score_scale = 1.0 / math.sqrt(head_size)
    group_queries = lax.dynamic_slice_in_dim(
        queries, kv_head * per_kv * head_size, per_kv * head_size, 1
    )
    group_queries = group_queries.astype(jnp.float32).reshape(seq_rows, per_kv, head_size)
    fresh_key = lax.dynamic_slice_in_dim(key_new, kv_head * head_size, head_size, 1).astype(
        jnp.float32
    )
    fresh_value = lax.dynamic_slice_in_dim(value_new, kv_head * head_size, head_size, 1).astype(
        jnp.float32
    )
    keys_here = key_cache[:, 0].astype(jnp.float32)
    values_here = value_cache[:, 0].astype(jnp.float32)
    scores = jnp.einsum("shd,spd->shp", group_queries, keys_here) * score_scale
    fresh_scores = jnp.einsum("shd,sd->sh", group_queries, fresh_key) * score_scale
    places = quarter * positions_here + jnp.arange(positions_here, dtype=jnp.int32)
    usable = (places[None, :] < lengths[:, None])[:, None, :]
    with_fresh = quarter == 0
    largest = jnp.maximum(
        jnp.max(jnp.where(usable, scores, -1e30), axis=2),
        jnp.where(with_fresh, fresh_scores, -1e30),
    )
    weights = jnp.where(usable, jnp.exp(scores - largest[..., None]), 0.0)
    fresh_weight = jnp.where(with_fresh, jnp.exp(fresh_scores - largest), 0.0)
    totals = jnp.sum(weights, axis=2) + fresh_weight
    weighted = (
        jnp.einsum("shp,spd->shd", weights, values_here)
        + fresh_weight[..., None] * fresh_value[:, None, :]
    )
    for bit_number in range(quarters.bit_length() - 1):
        peer_max, peer_total, peer_weighted = partner(
            (largest, totals, weighted), "blk", 1 << bit_number
        )
        merged = jnp.maximum(largest, peer_max)
        mine_factor = jnp.exp(largest - merged)
        peer_factor = jnp.exp(peer_max - merged)
        totals = totals * mine_factor + peer_total * peer_factor
        weighted = weighted * mine_factor[..., None] + peer_weighted * peer_factor[..., None]
        largest = merged
    attention = weighted / totals[..., None]
    own_output = lax.dynamic_slice_in_dim(attention, quarter * own_heads, own_heads, 1).reshape(
        seq_rows, own_heads * head_size
    )
    return residual_in.astype(jnp.float32) + own_output


def on_device(
    residual_in,
    queries,
    key_cache,
    value_cache,
    key_new,
    value_new,
    lengths,
    ffn_gain,
    gate_weight,
    up_weight,
    down_weight,
):
    groups = lax.axis_size("grp")
    group = lax.axis_index("grp")
    chips = lax.axis_size("blk") // 2
    chip, core = lax.axis_index("blk") // 2, lax.axis_index("blk") % 2
    rows = residual_in.shape[0]
    parts = 2 * chips // groups
    shard_rows = rows // parts

    wide = attend(residual_in, queries, key_cache, value_cache, key_new, value_new, lengths)

    tokens = (wide * ffn_gain.astype(jnp.float32)[None, :]).astype(jnp.bfloat16)
    blocks = [tokens] + [partner(tokens, "grp", i) for i in range(1, groups)]

    squares = jnp.sum(wide * wide, axis=1)
    for bit_number in range(lax.axis_size("blk").bit_length() - 1):
        squares = squares + partner(squares, "blk", 1 << bit_number)

    spot = jnp.where(chip % 2 == 1, (chip + 1) // 2, (chips - chip // 2) % chips)
    shard = jnp.arange(groups * parts, dtype=jnp.int32) ^ (group * parts)
    place = (spot - 1 - shard) % chips + jnp.where(shard // chips == core, 0, chips)
    own_shard = (core * chips + spot) ^ (group * parts)

    unit = gate_weight.shape[1] // sum(CHUNK_UNITS)
    edges = [sum(CHUNK_UNITS[:i]) for i in range(len(CHUNK_UNITS) + 1)]
    f32 = jnp.float32
    n_chunks = len(CHUNK_UNITS)
    inverse, total = None, None
    chunks = [{} for _ in range(n_chunks)]
    last = []

    order = [0, 2 * chips, 2 * chips - 1, *range(chips, 0, -1)]
    for turn in range(n_chunks + 2 * chips):
        for stage in order:
            k = turn - stage
            if stage == chips - 1:
                for j in range(1, chips - 1):
                    if 0 <= turn - chips - j < n_chunks:
                        last = last + [chunks[turn - chips - j]["hidden"][j]]
                if turn == 1:
                    last = last + squares
                    squares = jnp.stack(squares).reshape(groups * parts, shard_rows)
                    squares = lax.dynamic_index_in_dim(squares, own_shard, 0, keepdims=False)
                    inverse = lax.rsqrt(squares / D + 1e-05)[:, None]
            if not 0 <= k < n_chunks:
                continue
            units, chunk = CHUNK_UNITS[k], chunks[k]
            if stage == 0:
                ride = squares[None, :] if k == 0 else None
                keep, send, *rides = gate_up(
                    place, blocks, gate_weight, up_weight, unit, edges[k], units, last, ride
                )
                last = [keep]
                chunk.update(own=keep, flow=None)
                if k == 0:
                    squares = rides[0][0]
                    squares = [squares] + [partner(squares, "grp", i) for i in range(1, groups)]
            elif stage < chips:
                flow = pass_on(
                    stage - 1, chips, chunk["own"], chunk["other"], chunk["flow"], last
                )
                last = [flow]
                chunk["flow"] = along_ring(flow)
            elif stage == chips:
                hidden = hidden_units(chunk["flow"], chunk["own"], chunk["other"], inverse, last)
                last = [hidden]
                chunk["hidden"] = [hidden]
                for _ in range(1, chips):
                    chunk["hidden"].append(along_ring(chunk["hidden"][-1]))
            elif stage == 2 * chips - 1:
                ours = join(chunk["hidden"][1:] + chunk["hidden"][:1], last)
                last = [ours]
                chunk.update(ours=ours, theirs=partner(ours, "blk", 1))
            else:
                total, *terms = down(
                    place,
                    groups,
                    chunk["ours"],
                    chunk["theirs"],
                    down_weight,
                    total,
                    2 * unit,
                    edges[k] // 2,
                    units // 2,
                    last,
                    k == n_chunks - 1,
                )
                last = [total]
        if turn < n_chunks:
            send = hold(send, last) if turn > 0 else send
            last = [send]
            chunks[turn]["other"] = partner(send, "blk", 1)

    out = wide + total
    for i in range(1, groups):
        out = out + partner(terms[i - 1], "grp", i).astype(f32)
    return out


def solution(mesh):
    in_specs = (
        P("grp", "blk"),
        P("grp", None),
        P("grp", "blk", None, None),
        P("grp", "blk", None, None),
        P("grp", None),
        P("grp", None),
        P("grp"),
        P("blk"),
        P("blk", "grp"),
        P("blk", "grp"),
        P("grp", "blk"),
    )
    out_specs = P("grp", "blk")
    return jax.shard_map(
        on_device, mesh=mesh, in_specs=in_specs, out_specs=out_specs, check_vma=False
    )
```

```python
import functools
import math

import jax
import jax.numpy as jnp
from jax import lax
from jax.experimental import pallas as pl
from jax.experimental.pallas import tpu as pltpu
from jax.sharding import PartitionSpec as P

D = 16384
HEADS = 128
KV_HEADS = 8
CHUNK_UNITS = (8, 10, 8)
SLOTS = 4
VMEM = 38 * 1024 * 1024
SMALL_VMEM = 8 * 1024 * 1024


def partner(x, axis, distance):
    return lax.ppermute(x, axis, [(i, i ^ distance) for i in range(lax.axis_size(axis))])


def along_ring(x):
    chips = lax.axis_size("blk") // 2
    ring = [0, *range(1, chips, 2), *range(chips - 2, 0, -2)]
    hops = zip(ring, ring[1:] + ring[:1])
    return lax.ppermute(x, "blk", [(2 * a + c, 2 * b + c) for a, b in hops for c in range(2)])


def stream(units, copies, prepare, compute):
    def start(i, slot):
        for copy in copies(i, slot):
            copy.start()

    for i in range(min(2, units)):
        start(i, i)
    prepare()

    def step(i, _):
        slot = lax.rem(i, SLOTS)
        for copy in copies(i, slot):
            copy.wait()

        @pl.when(i == 0)
        def _():
            for later in range(2, min(SLOTS - 1, units)):
                start(later, later)

        later = i + SLOTS - 1

        @pl.when(later < units)
        def _():
            start(later, lax.rem(later, SLOTS))

        compute(i, slot)
        return 0

    lax.fori_loop(0, units, step, 0)


def gate_up_kernel(n_blocks, has_ride, first_unit, units, place_ref, *refs):
    blocks, gate_ref, up_ref = refs[:n_blocks], refs[n_blocks], refs[n_blocks + 1]
    keep_ref, send_ref, *rest = refs[-5 - has_ride :]
    x_ref, held, sems = rest[-3:]
    half = keep_ref.shape[1]
    unit = held.shape[3]
    parts = (place_ref.shape[0] - 1) // n_blocks
    rows = blocks[0].shape[0] // parts

    def copies(i, slot):
        columns = pl.ds(pl.multiple_of((first_unit + i) * unit, unit), unit)
        return [
            pltpu.make_async_copy(weight.at[:, columns], held.at[slot, j], sems.at[slot, j])
            for j, weight in enumerate((gate_ref, up_ref))
        ]

    def prepare():
        if has_ride:
            rest[0][...] = refs[n_blocks + 2][...]
        for i in range(n_blocks * parts):
            to = pl.ds(pl.multiple_of(place_ref[i] * rows, rows), rows)
            x_ref[to, :] = blocks[i // parts][i % parts * rows : (i % parts + 1) * rows, :]

    def compute(i, slot):
        columns = pl.ds(pl.multiple_of(i * unit, unit), unit)
        for j in range(2):
            y = jnp.dot(x_ref[...], held[slot, j], preferred_element_type=jnp.float32)
            keep_ref[j, :, columns] = y[:half].astype(jnp.bfloat16)
            send_ref[j, :, columns] = y[half:].astype(jnp.bfloat16)

    stream(units, copies, prepare, compute)


def gate_up(place, blocks, gate_weight, up_weight, unit, start, units, after, ride=None):
    rows, depth = blocks[0].shape
    total = rows * len(blocks)
    cols = units * unit
    rides = [] if ride is None else [ride]
    vmem = pl.BlockSpec(memory_space=pltpu.VMEM)
    anywhere = pl.BlockSpec(memory_space=pl.ANY)
    return pl.pallas_call(
        functools.partial(gate_up_kernel, len(blocks), len(rides), start, units),
        in_specs=[pl.BlockSpec(memory_space=pltpu.SMEM)]
        + [vmem] * len(blocks)
        + [pl.BlockSpec(memory_space=pltpu.HBM)] * 2
        + [vmem] * len(rides)
        + [anywhere] * len(after),
        out_specs=[vmem] * (2 + len(rides)),
        out_shape=[jax.ShapeDtypeStruct((2, total // 2, cols), jnp.bfloat16)] * 2
        + [jax.ShapeDtypeStruct(r.shape, r.dtype) for r in rides],
        scratch_shapes=[
            pltpu.VMEM((total, depth), jnp.bfloat16),
            pltpu.VMEM((SLOTS, 2, depth, unit), jnp.bfloat16),
            pltpu.SemaphoreType.DMA((SLOTS, 2)),
        ],
        compiler_params=pltpu.CompilerParams(vmem_limit_bytes=VMEM),
        cost_estimate=pl.CostEstimate(
            flops=4 * total * depth * cols,
            bytes_accessed=4 * depth * cols + 2 * total * depth + 4 * total * cols,
            transcendentals=0,
        ),
    )(place, *blocks, gate_weight, up_weight, *rides, *after)


def nothing(*refs):
    pass


def hold(x, after):
    anywhere = pl.BlockSpec(memory_space=pl.ANY)
    return pl.pallas_call(
        nothing,
        in_specs=[anywhere] * (1 + len(after)),
        out_specs=anywhere,
        out_shape=jax.ShapeDtypeStruct(x.shape, x.dtype),
        input_output_aliases={0: 0},
        compiler_params=pltpu.CompilerParams(vmem_limit_bytes=SMALL_VMEM),
        cost_estimate=pl.CostEstimate(flops=0, bytes_accessed=0, transcendentals=0),
    )(x, *after)


def pass_on_kernel(shard, has_flow, own_ref, other_ref, *refs):
    out_ref = refs[-1]
    rows = out_ref.shape[1]
    here = slice(shard * rows, (shard + 1) * rows)
    total = own_ref[:, here].astype(jnp.float32) + other_ref[:, here].astype(jnp.float32)
    if has_flow:
        total = total + refs[0][...].astype(jnp.float32)
    out_ref[...] = total.astype(jnp.bfloat16)


def pass_on(shard, shards, own, other, flow, after):
    vmem = pl.BlockSpec(memory_space=pltpu.VMEM)
    flows = [] if flow is None else [flow]
    return pl.pallas_call(
        functools.partial(pass_on_kernel, shard, len(flows)),
        in_specs=[vmem] * (2 + len(flows)) + [pl.BlockSpec(memory_space=pl.ANY)] * len(after),
        out_specs=vmem,
        out_shape=jax.ShapeDtypeStruct(
            (2, own.shape[1] // shards, own.shape[2]), jnp.bfloat16
        ),
        compiler_params=pltpu.CompilerParams(vmem_limit_bytes=SMALL_VMEM),
        cost_estimate=pl.CostEstimate(
            flops=2 * own.size // shards, bytes_accessed=8 * own.size // shards, transcendentals=0
        ),
    )(own, other, *flows, *after)


def hidden_kernel(n_squares, width, place_ref, flow_ref, own_ref, other_ref, *refs):
    squares, out_ref, all_ref = refs[:n_squares], refs[-2], refs[-1]
    rows = flow_ref.shape[1]
    for i, square in enumerate(squares):
        all_ref[i * square.shape[0] : (i + 1) * square.shape[0]] = square[...]
    here = pl.ds(pl.multiple_of(place_ref[place_ref.shape[0] - 1] * rows, rows), rows)
    inverse = lax.rsqrt(all_ref[here, :] / width + 1e-05)
    gate, up = [
        (
            own_ref[i, -rows:].astype(jnp.float32)
            + other_ref[i, -rows:].astype(jnp.float32)
            + flow_ref[i].astype(jnp.float32)
        )
        * inverse
        for i in range(2)
    ]
    out_ref[...] = (gate / (1 + jnp.exp(-gate)) * up).astype(jnp.bfloat16)


def hidden_units(place, flow, own, other, squares, after):
    _, rows, cols = flow.shape
    vmem = pl.BlockSpec(memory_space=pltpu.VMEM)
    return pl.pallas_call(
        functools.partial(hidden_kernel, len(squares), D),
        in_specs=[pl.BlockSpec(memory_space=pltpu.SMEM)]
        + [vmem] * (3 + len(squares))
        + [pl.BlockSpec(memory_space=pl.ANY)] * len(after),
        out_specs=vmem,
        out_shape=jax.ShapeDtypeStruct((rows, cols), jnp.bfloat16),
        scratch_shapes=[pltpu.VMEM((len(squares) * squares[0].shape[0], 1), jnp.float32)],
        compiler_params=pltpu.CompilerParams(vmem_limit_bytes=SMALL_VMEM),
        cost_estimate=pl.CostEstimate(
            flops=16 * rows * cols, bytes_accessed=14 * rows * cols, transcendentals=rows * cols
        ),
    )(place, flow, own, other, *squares, *after)


def join_kernel(n_shards, *refs):
    out_ref = refs[-1]
    rows = refs[0].shape[0]
    for i, shard in enumerate(refs[:n_shards]):
        out_ref[i * rows : (i + 1) * rows] = shard[...]


def join(shards, after):
    rows, cols = shards[0].shape
    vmem = pl.BlockSpec(memory_space=pltpu.VMEM)
    return pl.pallas_call(
        functools.partial(join_kernel, len(shards)),
        in_specs=[vmem] * len(shards) + [pl.BlockSpec(memory_space=pl.ANY)] * len(after),
        out_specs=vmem,
        out_shape=jax.ShapeDtypeStruct((rows * len(shards), cols), jnp.bfloat16),
        compiler_params=pltpu.CompilerParams(vmem_limit_bytes=SMALL_VMEM),
        cost_estimate=pl.CostEstimate(
            flops=0, bytes_accessed=4 * rows * len(shards) * cols, transcendentals=0
        ),
    )(*shards, *after)


def down_kernel(has_total, n_outs, first_unit, units, place_ref, *refs):
    ours_ref, theirs_ref, weight_ref = refs[:3]
    is_last = n_outs > 1
    x_ref, held, sems, *rest = refs[len(refs) - 3 - is_last :]
    outs = refs[len(refs) - 3 - is_last - n_outs : len(refs) - 3 - is_last]
    total_ref = rest[0] if is_last else outs[0]
    half = ours_ref.shape[0]
    unit = held.shape[1]

    def copies(i, slot):
        here = pl.ds(pl.multiple_of((first_unit + i) * unit, unit), unit)
        return [pltpu.make_async_copy(weight_ref.at[here, :], held.at[slot], sems.at[slot])]

    def prepare():
        x_ref[:half] = ours_ref[...]
        x_ref[half:] = theirs_ref[...]
        total_ref[...] = refs[3][...] if has_total else jnp.zeros_like(total_ref)

    def compute(i, slot):
        x = x_ref[:, pl.ds(pl.multiple_of(i * unit, unit), unit)]
        total_ref[...] += jnp.dot(x, held[slot], preferred_element_type=jnp.float32)

    stream(units, copies, prepare, compute)
    if is_last:
        parts = (place_ref.shape[0] - 1) // n_outs
        for i in range(n_outs * parts):
            out_ref = outs[i // parts]
            rows = out_ref.shape[0] // parts
            term = total_ref[pl.ds(pl.multiple_of(place_ref[i] * rows, rows), rows), :]
            out_ref[i % parts * rows : (i % parts + 1) * rows, :] = term.astype(out_ref.dtype)


def down(place, groups, ours, theirs, weight, total, unit, start, units, after, is_last):
    half, cols = ours.shape
    width = weight.shape[1]
    has_total = total is not None
    vmem = pl.BlockSpec(memory_space=pltpu.VMEM)
    rows = 2 * half // groups
    outs = [jax.ShapeDtypeStruct((2 * half, width), jnp.float32)]
    if is_last:
        outs = [jax.ShapeDtypeStruct((rows, width), jnp.float32)]
        outs += [jax.ShapeDtypeStruct((rows, width), jnp.bfloat16)] * (groups - 1)
    return pl.pallas_call(
        functools.partial(down_kernel, has_total, len(outs), start, units),
        in_specs=[pl.BlockSpec(memory_space=pltpu.SMEM), vmem, vmem]
        + [pl.BlockSpec(memory_space=pltpu.HBM)]
        + [vmem] * has_total
        + [pl.BlockSpec(memory_space=pl.ANY)] * len(after),
        out_specs=[vmem] * len(outs),
        out_shape=outs,
        scratch_shapes=[
            pltpu.VMEM((2 * half, cols), jnp.bfloat16),
            pltpu.VMEM((SLOTS, unit, width), jnp.bfloat16),
            pltpu.SemaphoreType.DMA((SLOTS,)),
        ]
        + [pltpu.VMEM((2 * half, width), jnp.float32)] * is_last,
        compiler_params=pltpu.CompilerParams(vmem_limit_bytes=VMEM),
        cost_estimate=pl.CostEstimate(
            flops=4 * half * units * unit * width,
            bytes_accessed=2 * units * unit * width + 16 * half * width,
            transcendentals=0,
        ),
    )(place, ours, theirs, weight, *([total] if has_total else []), *after)


def attend(residual_in, queries, key_cache, value_cache, key_new, value_new, lengths):
    cycle_size = lax.axis_size("blk")
    quarters = cycle_size // KV_HEADS
    per_kv = HEADS // KV_HEADS
    own_heads = HEADS // cycle_size
    head_size = key_cache.shape[3]
    seq_rows = residual_in.shape[0]
    positions_here = key_cache.shape[2]
    blk_index = lax.axis_index("blk")
    kv_head = blk_index // quarters
    quarter = blk_index % quarters
    score_scale = 1.0 / math.sqrt(head_size)
    group_queries = lax.dynamic_slice_in_dim(
        queries, kv_head * per_kv * head_size, per_kv * head_size, 1
    )
    group_queries = group_queries.astype(jnp.float32).reshape(seq_rows, per_kv, head_size)
    fresh_key = lax.dynamic_slice_in_dim(key_new, kv_head * head_size, head_size, 1).astype(
        jnp.float32
    )
    fresh_value = lax.dynamic_slice_in_dim(value_new, kv_head * head_size, head_size, 1).astype(
        jnp.float32
    )
    keys_here = key_cache[:, 0].astype(jnp.float32)
    values_here = value_cache[:, 0].astype(jnp.float32)
    scores = jnp.einsum("shd,spd->shp", group_queries, keys_here) * score_scale
    fresh_scores = jnp.einsum("shd,sd->sh", group_queries, fresh_key) * score_scale
    places = quarter * positions_here + jnp.arange(positions_here, dtype=jnp.int32)
    usable = (places[None, :] < lengths[:, None])[:, None, :]
    with_fresh = quarter == 0
    largest = jnp.maximum(
        jnp.max(jnp.where(usable, scores, -1e30), axis=2),
        jnp.where(with_fresh, fresh_scores, -1e30),
    )
    weights = jnp.where(usable, jnp.exp(scores - largest[..., None]), 0.0)
    fresh_weight = jnp.where(with_fresh, jnp.exp(fresh_scores - largest), 0.0)
    totals = jnp.sum(weights, axis=2) + fresh_weight
    weighted = (
        jnp.einsum("shp,spd->shd", weights, values_here)
        + fresh_weight[..., None] * fresh_value[:, None, :]
    )
    for bit_number in range(quarters.bit_length() - 1):
        peer_max, peer_total, peer_weighted = partner(
            (largest, totals, weighted), "blk", 1 << bit_number
        )
        merged = jnp.maximum(largest, peer_max)
        mine_factor = jnp.exp(largest - merged)
        peer_factor = jnp.exp(peer_max - merged)
        totals = totals * mine_factor + peer_total * peer_factor
        weighted = weighted * mine_factor[..., None] + peer_weighted * peer_factor[..., None]
        largest = merged
    attention = weighted / totals[..., None]
    own_output = lax.dynamic_slice_in_dim(attention, quarter * own_heads, own_heads, 1).reshape(
        seq_rows, own_heads * head_size
    )
    return residual_in.astype(jnp.float32) + own_output


def on_device(
    residual_in,
    queries,
    key_cache,
    value_cache,
    key_new,
    value_new,
    lengths,
    ffn_gain,
    gate_weight,
    up_weight,
    down_weight,
):
    groups = lax.axis_size("grp")
    group = lax.axis_index("grp")
    chips = lax.axis_size("blk") // 2
    chip, core = lax.axis_index("blk") // 2, lax.axis_index("blk") % 2
    rows = residual_in.shape[0]
    parts = 2 * chips // groups

    wide = attend(residual_in, queries, key_cache, value_cache, key_new, value_new, lengths)

    tokens = (wide * ffn_gain.astype(jnp.float32)[None, :]).astype(jnp.bfloat16)
    blocks = [tokens] + [partner(tokens, "grp", i) for i in range(1, groups)]

    squares = jnp.sum(wide * wide, axis=1, keepdims=True)
    for bit_number in range(lax.axis_size("blk").bit_length() - 1):
        squares = squares + partner(squares, "blk", 1 << bit_number)

    spot = jnp.where(chip % 2 == 1, (chip + 1) // 2, (chips - chip // 2) % chips)
    shard = jnp.arange(groups * parts, dtype=jnp.int32) ^ (group * parts)
    place = (spot - 1 - shard) % chips + jnp.where(shard // chips == core, 0, chips)
    own_shard = (core * chips + spot) ^ (group * parts)
    place = jnp.concatenate([place, own_shard[None]]).astype(jnp.int32)

    unit = gate_weight.shape[1] // sum(CHUNK_UNITS)
    edges = [sum(CHUNK_UNITS[:i]) for i in range(len(CHUNK_UNITS) + 1)]
    f32 = jnp.float32
    n_chunks = len(CHUNK_UNITS)
    total = None
    chunks = [{} for _ in range(n_chunks)]
    last = []

    flowing = [0, 2 * chips, 2 * chips - 1, chips, None, *range(chips - 1, 0, -1)]
    closing = [2 * chips, None, 2 * chips - 1]
    for turn in range(n_chunks + 2 * chips):
        for stage in flowing if turn < n_chunks + chips else closing:
            if stage is None:
                for j in range(1, chips - 1):
                    if 0 <= turn - chips - j < n_chunks:
                        last = last + [chunks[turn - chips - j]["hidden"][j]]
                if turn == 1:
                    last = last + squares
                continue
            k = turn - stage
            if not 0 <= k < n_chunks:
                continue
            units, chunk = CHUNK_UNITS[k], chunks[k]
            if stage == 0:
                ride = squares if k == 0 else None
                keep, send, *rides = gate_up(
                    place, blocks, gate_weight, up_weight, unit, edges[k], units, last, ride
                )
                last = [keep]
                chunk.update(own=keep, flow=None)
                if k == 0:
                    squares = rides[0]
                    squares = [squares] + [partner(squares, "grp", i) for i in range(1, groups)]
            elif stage < chips:
                flow = pass_on(
                    stage - 1, chips, chunk["own"], chunk["other"], chunk["flow"], last
                )
                last = [flow]
                chunk["flow"] = along_ring(flow)
            elif stage == chips:
                hidden = hidden_units(
                    place, chunk["flow"], chunk["own"], chunk["other"], squares, last
                )
                last = [hidden]
                chunk["hidden"] = [hidden]
                for _ in range(1, chips):
                    chunk["hidden"].append(along_ring(chunk["hidden"][-1]))
            elif stage == 2 * chips - 1:
                ours = join(chunk["hidden"][1:] + chunk["hidden"][:1], last)
                last = [ours]
                chunk.update(ours=ours, theirs=partner(ours, "blk", 1))
            else:
                total, *terms = down(
                    place,
                    groups,
                    chunk["ours"],
                    chunk["theirs"],
                    down_weight,
                    total,
                    2 * unit,
                    edges[k] // 2,
                    units // 2,
                    last,
                    k == n_chunks - 1,
                )
                last = [total]
        if turn < n_chunks:
            send = hold(send, last) if turn > 0 else send
            last = [send]
            chunks[turn]["other"] = partner(send, "blk", 1)

    out = wide + total
    for i in range(1, groups):
        out = out + partner(terms[i - 1], "grp", i).astype(f32)
    return out


def solution(mesh):
    in_specs = (
        P("grp", "blk"),
        P("grp", None),
        P("grp", "blk", None, None),
        P("grp", "blk", None, None),
        P("grp", None),
        P("grp", None),
        P("grp"),
        P("blk"),
        P("blk", "grp"),
        P("blk", "grp"),
        P("grp", "blk"),
    )
    out_specs = P("grp", "blk")
    return jax.shard_map(
        on_device, mesh=mesh, in_specs=in_specs, out_specs=out_specs, check_vma=False
    )
```

```python
import functools
import math

import jax
import jax.numpy as jnp
from jax import lax
from jax.experimental import pallas as pl
from jax.experimental.pallas import tpu as pltpu
from jax.sharding import PartitionSpec as P

D = 16384
HEADS = 128
KV_HEADS = 8
CHUNK_UNITS = (8, 12, 6)
SLOTS = 4
READY = 2
READY_DOWN = 1
VMEM = 38 * 1024 * 1024
SMALL_VMEM = 8 * 1024 * 1024


def partner(x, axis, distance):
    return lax.ppermute(x, axis, [(i, i ^ distance) for i in range(lax.axis_size(axis))])


def along_ring(x):
    chips = lax.axis_size("blk") // 2
    ring = [0, *range(1, chips, 2), *range(chips - 2, 0, -2)]
    hops = zip(ring, ring[1:] + ring[:1])
    return lax.ppermute(x, "blk", [(2 * a + c, 2 * b + c) for a, b in hops for c in range(2)])


def stream(units, ready, copies, ahead, prepare, compute):
    ready = min(ready, units)
    streamed = units - ready

    def start(i, slot):
        for copy in copies(ready + i, slot):
            copy.start()

    for i in range(min(2, streamed)):
        start(i, i)
    prepare()
    for i in range(ready):
        compute(i, None)

    def step(i, _):
        slot = lax.rem(i, SLOTS)
        for copy in copies(ready + i, slot):
            copy.wait()

        @pl.when(i == 0)
        def _():
            for later in range(2, min(SLOTS - 1, streamed)):
                start(later, later)

        later = i + SLOTS - 1

        @pl.when(later < streamed)
        def _():
            start(later, lax.rem(later, SLOTS))

        @pl.when(i == max(streamed - SLOTS + 1, 0))
        def _():
            for copy in ahead:
                copy.start()

        compute(ready + i, slot)
        return 0

    lax.fori_loop(0, streamed, step, 0)
    for copy in ahead:
        copy.wait()


def bring_kernel(n_weights, first_unit, by_rows, *refs):
    weights, out_ref, sems = refs[:n_weights], refs[-2], refs[-1]
    copies = tiles(weights, out_ref, sems, first_unit, by_rows)
    for copy in copies:
        copy.start()
    for copy in copies:
        copy.wait()


def tiles(weights, out_ref, sems, first_unit, by_rows):
    count, unit = out_ref.shape[0], out_ref.shape[1 if by_rows else 3]
    copies = []
    for i in range(count):
        here = slice((first_unit + i) * unit, (first_unit + i + 1) * unit)
        for j, weight in enumerate(weights):
            source = weight.at[here, :] if by_rows else weight.at[:, here]
            target = out_ref.at[i] if by_rows else out_ref.at[i, j]
            copies.append(pltpu.make_async_copy(source, target, sems.at[i, j]))
    return copies


def bring(weights, shape, first_unit, by_rows, after):
    return pl.pallas_call(
        functools.partial(bring_kernel, len(weights), first_unit, by_rows),
        in_specs=[pl.BlockSpec(memory_space=pltpu.HBM)] * len(weights)
        + [pl.BlockSpec(memory_space=pl.ANY)] * len(after),
        out_specs=pl.BlockSpec(memory_space=pltpu.VMEM),
        out_shape=jax.ShapeDtypeStruct(shape, jnp.bfloat16),
        scratch_shapes=[pltpu.SemaphoreType.DMA((shape[0], len(weights)))],
        compiler_params=pltpu.CompilerParams(vmem_limit_bytes=VMEM),
        cost_estimate=pl.CostEstimate(
            flops=0, bytes_accessed=4 * math.prod(shape), transcendentals=0
        ),
    )(*weights, *after)


def gate_up_kernel(n_blocks, has_ride, has_next, first_unit, units, place_ref, *refs):
    blocks, (gate_ref, up_ref, ready_ref) = refs[:n_blocks], refs[n_blocks : n_blocks + 3]
    keep_ref, send_ref, *rest = refs[len(refs) - 6 - has_ride - has_next :]
    x_ref, held, sems, next_sems = rest[-4:]
    half = keep_ref.shape[1]
    unit = held.shape[3]
    parts = (place_ref.shape[0] - 1) // n_blocks
    rows = blocks[0].shape[0] // parts
    ahead = []
    if has_next:
        ahead = tiles((gate_ref, up_ref), rest[has_ride], next_sems, first_unit + units, False)

    def copies(i, slot):
        columns = pl.ds(pl.multiple_of((first_unit + i) * unit, unit), unit)
        return [
            pltpu.make_async_copy(weight.at[:, columns], held.at[slot, j], sems.at[slot, j])
            for j, weight in enumerate((gate_ref, up_ref))
        ]

    def prepare():
        if has_ride:
            rest[0][...] = refs[n_blocks + 3][...]
        for i in range(n_blocks * parts):
            to = pl.ds(pl.multiple_of(place_ref[i] * rows, rows), rows)
            x_ref[to, :] = blocks[i // parts][i % parts * rows : (i % parts + 1) * rows, :]

    def compute(i, slot):
        columns = pl.ds(i * unit if slot is None else pl.multiple_of(i * unit, unit), unit)
        for j in range(2):
            weight = ready_ref[i, j] if slot is None else held[slot, j]
            y = jnp.dot(x_ref[...], weight, preferred_element_type=jnp.float32)
            keep_ref[j, :, columns] = y[:half].astype(jnp.bfloat16)
            send_ref[j, :, columns] = y[half:].astype(jnp.bfloat16)

    stream(units, ready_ref.shape[0], copies, ahead, prepare, compute)


def gate_up(
    place, blocks, gate_weight, up_weight, ready, unit, start, units, after, has_next, ride=None
):
    rows, depth = blocks[0].shape
    total = rows * len(blocks)
    cols = units * unit
    rides = [] if ride is None else [ride]
    vmem = pl.BlockSpec(memory_space=pltpu.VMEM)
    outs = [jax.ShapeDtypeStruct((2, total // 2, cols), jnp.bfloat16)] * 2
    outs += [jax.ShapeDtypeStruct(r.shape, r.dtype) for r in rides]
    outs += [jax.ShapeDtypeStruct(ready.shape, ready.dtype)] * has_next
    return pl.pallas_call(
        functools.partial(gate_up_kernel, len(blocks), len(rides), has_next, start, units),
        in_specs=[pl.BlockSpec(memory_space=pltpu.SMEM)]
        + [vmem] * len(blocks)
        + [pl.BlockSpec(memory_space=pltpu.HBM)] * 2
        + [vmem] * (1 + len(rides))
        + [pl.BlockSpec(memory_space=pl.ANY)] * len(after),
        out_specs=[vmem] * len(outs),
        out_shape=outs,
        scratch_shapes=[
            pltpu.VMEM((total, depth), jnp.bfloat16),
            pltpu.VMEM((SLOTS, 2, depth, unit), jnp.bfloat16),
            pltpu.SemaphoreType.DMA((SLOTS, 2)),
            pltpu.SemaphoreType.DMA((READY, 2)),
        ],
        compiler_params=pltpu.CompilerParams(vmem_limit_bytes=VMEM),
        cost_estimate=pl.CostEstimate(
            flops=4 * total * depth * cols,
            bytes_accessed=4 * depth * cols + 2 * total * depth + 4 * total * cols,
            transcendentals=0,
        ),
    )(place, *blocks, gate_weight, up_weight, ready, *rides, *after)


def nothing(*refs):
    pass


def hold(x, after):
    anywhere = pl.BlockSpec(memory_space=pl.ANY)
    return pl.pallas_call(
        nothing,
        in_specs=[anywhere] * (1 + len(after)),
        out_specs=anywhere,
        out_shape=jax.ShapeDtypeStruct(x.shape, x.dtype),
        input_output_aliases={0: 0},
        compiler_params=pltpu.CompilerParams(vmem_limit_bytes=SMALL_VMEM),
        cost_estimate=pl.CostEstimate(flops=0, bytes_accessed=0, transcendentals=0),
    )(x, *after)


def pass_on_kernel(shard, has_flow, own_ref, other_ref, *refs):
    out_ref = refs[-1]
    rows = out_ref.shape[1]
    here = slice(shard * rows, (shard + 1) * rows)
    total = own_ref[:, here].astype(jnp.float32) + other_ref[:, here].astype(jnp.float32)
    if has_flow:
        total = total + refs[0][...].astype(jnp.float32)
    out_ref[...] = total.astype(jnp.bfloat16)


def pass_on(shard, shards, own, other, flow, after):
    vmem = pl.BlockSpec(memory_space=pltpu.VMEM)
    flows = [] if flow is None else [flow]
    return pl.pallas_call(
        functools.partial(pass_on_kernel, shard, len(flows)),
        in_specs=[vmem] * (2 + len(flows)) + [pl.BlockSpec(memory_space=pl.ANY)] * len(after),
        out_specs=vmem,
        out_shape=jax.ShapeDtypeStruct(
            (2, own.shape[1] // shards, own.shape[2]), jnp.bfloat16
        ),
        compiler_params=pltpu.CompilerParams(vmem_limit_bytes=SMALL_VMEM),
        cost_estimate=pl.CostEstimate(
            flops=2 * own.size // shards, bytes_accessed=8 * own.size // shards, transcendentals=0
        ),
    )(own, other, *flows, *after)


def hidden_kernel(n_squares, width, place_ref, flow_ref, own_ref, other_ref, *refs):
    squares, out_ref, all_ref = refs[:n_squares], refs[-2], refs[-1]
    rows = flow_ref.shape[1]
    for i, square in enumerate(squares):
        all_ref[i * square.shape[0] : (i + 1) * square.shape[0]] = square[...]
    here = pl.ds(pl.multiple_of(place_ref[place_ref.shape[0] - 1] * rows, rows), rows)
    inverse = lax.rsqrt(all_ref[here, :] / width + 1e-05)
    gate, up = [
        (
            own_ref[i, -rows:].astype(jnp.float32)
            + other_ref[i, -rows:].astype(jnp.float32)
            + flow_ref[i].astype(jnp.float32)
        )
        * inverse
        for i in range(2)
    ]
    out_ref[...] = (gate / (1 + jnp.exp(-gate)) * up).astype(jnp.bfloat16)


def hidden_units(place, flow, own, other, squares, after):
    _, rows, cols = flow.shape
    vmem = pl.BlockSpec(memory_space=pltpu.VMEM)
    return pl.pallas_call(
        functools.partial(hidden_kernel, len(squares), D),
        in_specs=[pl.BlockSpec(memory_space=pltpu.SMEM)]
        + [vmem] * (3 + len(squares))
        + [pl.BlockSpec(memory_space=pl.ANY)] * len(after),
        out_specs=vmem,
        out_shape=jax.ShapeDtypeStruct((rows, cols), jnp.bfloat16),
        scratch_shapes=[pltpu.VMEM((len(squares) * squares[0].shape[0], 1), jnp.float32)],
        compiler_params=pltpu.CompilerParams(vmem_limit_bytes=SMALL_VMEM),
        cost_estimate=pl.CostEstimate(
            flops=16 * rows * cols, bytes_accessed=14 * rows * cols, transcendentals=rows * cols
        ),
    )(place, flow, own, other, *squares, *after)


def join_kernel(n_shards, *refs):
    out_ref = refs[-1]
    rows = refs[0].shape[0]
    for i, shard in enumerate(refs[:n_shards]):
        out_ref[i * rows : (i + 1) * rows] = shard[...]


def join(shards, after):
    rows, cols = shards[0].shape
    vmem = pl.BlockSpec(memory_space=pltpu.VMEM)
    return pl.pallas_call(
        functools.partial(join_kernel, len(shards)),
        in_specs=[vmem] * len(shards) + [pl.BlockSpec(memory_space=pl.ANY)] * len(after),
        out_specs=vmem,
        out_shape=jax.ShapeDtypeStruct((rows * len(shards), cols), jnp.bfloat16),
        compiler_params=pltpu.CompilerParams(vmem_limit_bytes=SMALL_VMEM),
        cost_estimate=pl.CostEstimate(
            flops=0, bytes_accessed=4 * rows * len(shards) * cols, transcendentals=0
        ),
    )(*shards, *after)


def down_kernel(has_total, n_outs, first_unit, units, place_ref, *refs):
    ours_ref, theirs_ref, weight_ref, ready_ref = refs[:4]
    is_last = n_outs > 2
    x_ref, held, sems, next_sems, *rest = refs[len(refs) - 4 - is_last :]
    outs = refs[len(refs) - 4 - is_last - n_outs : len(refs) - 4 - is_last]
    total_ref = rest[0] if is_last else outs[0]
    half = ours_ref.shape[0]
    unit = held.shape[1]
    ahead = [] if is_last else tiles((weight_ref,), outs[1], next_sems, first_unit + units, True)

    def copies(i, slot):
        here = pl.ds(pl.multiple_of((first_unit + i) * unit, unit), unit)
        return [pltpu.make_async_copy(weight_ref.at[here, :], held.at[slot], sems.at[slot])]

    def prepare():
        x_ref[:half] = ours_ref[...]
        x_ref[half:] = theirs_ref[...]
        total_ref[...] = refs[4][...] if has_total else jnp.zeros_like(total_ref)

    def compute(i, slot):
        columns = pl.ds(i * unit if slot is None else pl.multiple_of(i * unit, unit), unit)
        weight = ready_ref[i] if slot is None else held[slot]
        total_ref[...] += jnp.dot(x_ref[:, columns], weight, preferred_element_type=jnp.float32)

    stream(units, ready_ref.shape[0], copies, ahead, prepare, compute)
    if is_last:
        parts = (place_ref.shape[0] - 1) // n_outs
        for i in range(n_outs * parts):
            out_ref = outs[i // parts]
            rows = out_ref.shape[0] // parts
            term = total_ref[pl.ds(pl.multiple_of(place_ref[i] * rows, rows), rows), :]
            out_ref[i % parts * rows : (i % parts + 1) * rows, :] = term.astype(out_ref.dtype)


def down(place, groups, ours, theirs, weight, ready, total, unit, start, units, after, is_last):
    half, cols = ours.shape
    width = weight.shape[1]
    has_total = total is not None
    vmem = pl.BlockSpec(memory_space=pltpu.VMEM)
    rows = 2 * half // groups
    outs = [
        jax.ShapeDtypeStruct((2 * half, width), jnp.float32),
        jax.ShapeDtypeStruct(ready.shape, ready.dtype),
    ]
    if is_last:
        outs = [jax.ShapeDtypeStruct((rows, width), jnp.float32)]
        outs += [jax.ShapeDtypeStruct((rows, width), jnp.bfloat16)] * (groups - 1)
    return pl.pallas_call(
        functools.partial(down_kernel, has_total, len(outs), start, units),
        in_specs=[pl.BlockSpec(memory_space=pltpu.SMEM), vmem, vmem]
        + [pl.BlockSpec(memory_space=pltpu.HBM), vmem]
        + [vmem] * has_total
        + [pl.BlockSpec(memory_space=pl.ANY)] * len(after),
        out_specs=[vmem] * len(outs),
        out_shape=outs,
        scratch_shapes=[
            pltpu.VMEM((2 * half, cols), jnp.bfloat16),
            pltpu.VMEM((SLOTS, unit, width), jnp.bfloat16),
            pltpu.SemaphoreType.DMA((SLOTS,)),
            pltpu.SemaphoreType.DMA((READY_DOWN, 1)),
        ]
        + [pltpu.VMEM((2 * half, width), jnp.float32)] * is_last,
        compiler_params=pltpu.CompilerParams(vmem_limit_bytes=VMEM),
        cost_estimate=pl.CostEstimate(
            flops=4 * half * units * unit * width,
            bytes_accessed=2 * units * unit * width + 16 * half * width,
            transcendentals=0,
        ),
    )(place, ours, theirs, weight, ready, *([total] if has_total else []), *after)


def attend(residual_in, queries, key_cache, value_cache, key_new, value_new, lengths):
    cycle_size = lax.axis_size("blk")
    quarters = cycle_size // KV_HEADS
    per_kv = HEADS // KV_HEADS
    own_heads = HEADS // cycle_size
    head_size = key_cache.shape[3]
    seq_rows = residual_in.shape[0]
    positions_here = key_cache.shape[2]
    blk_index = lax.axis_index("blk")
    kv_head = blk_index // quarters
    quarter = blk_index % quarters
    score_scale = 1.0 / math.sqrt(head_size)
    group_queries = lax.dynamic_slice_in_dim(
        queries, kv_head * per_kv * head_size, per_kv * head_size, 1
    )
    group_queries = group_queries.astype(jnp.float32).reshape(seq_rows, per_kv, head_size)
    fresh_key = lax.dynamic_slice_in_dim(key_new, kv_head * head_size, head_size, 1).astype(
        jnp.float32
    )
    fresh_value = lax.dynamic_slice_in_dim(value_new, kv_head * head_size, head_size, 1).astype(
        jnp.float32
    )
    keys_here = key_cache[:, 0].astype(jnp.float32)
    values_here = value_cache[:, 0].astype(jnp.float32)
    scores = jnp.einsum("shd,spd->shp", group_queries, keys_here) * score_scale
    fresh_scores = jnp.einsum("shd,sd->sh", group_queries, fresh_key) * score_scale
    places = quarter * positions_here + jnp.arange(positions_here, dtype=jnp.int32)
    usable = (places[None, :] < lengths[:, None])[:, None, :]
    with_fresh = quarter == 0
    largest = jnp.maximum(
        jnp.max(jnp.where(usable, scores, -1e30), axis=2),
        jnp.where(with_fresh, fresh_scores, -1e30),
    )
    weights = jnp.where(usable, jnp.exp(scores - largest[..., None]), 0.0)
    fresh_weight = jnp.where(with_fresh, jnp.exp(fresh_scores - largest), 0.0)
    totals = jnp.sum(weights, axis=2) + fresh_weight
    weighted = (
        jnp.einsum("shp,spd->shd", weights, values_here)
        + fresh_weight[..., None] * fresh_value[:, None, :]
    )
    for bit_number in range(quarters.bit_length() - 1):
        peer_max, peer_total, peer_weighted = partner(
            (largest, totals, weighted), "blk", 1 << bit_number
        )
        merged = jnp.maximum(largest, peer_max)
        mine_factor = jnp.exp(largest - merged)
        peer_factor = jnp.exp(peer_max - merged)
        totals = totals * mine_factor + peer_total * peer_factor
        weighted = weighted * mine_factor[..., None] + peer_weighted * peer_factor[..., None]
        largest = merged
    attention = weighted / totals[..., None]
    own_output = lax.dynamic_slice_in_dim(attention, quarter * own_heads, own_heads, 1).reshape(
        seq_rows, own_heads * head_size
    )
    return residual_in.astype(jnp.float32) + own_output


def on_device(
    residual_in,
    queries,
    key_cache,
    value_cache,
    key_new,
    value_new,
    lengths,
    ffn_gain,
    gate_weight,
    up_weight,
    down_weight,
):
    groups = lax.axis_size("grp")
    group = lax.axis_index("grp")
    chips = lax.axis_size("blk") // 2
    chip, core = lax.axis_index("blk") // 2, lax.axis_index("blk") % 2
    rows = residual_in.shape[0]
    parts = 2 * chips // groups

    wide = attend(residual_in, queries, key_cache, value_cache, key_new, value_new, lengths)

    tokens = (wide * ffn_gain.astype(jnp.float32)[None, :]).astype(jnp.bfloat16)
    blocks = [tokens] + [partner(tokens, "grp", i) for i in range(1, groups)]

    squares = jnp.sum(wide * wide, axis=1, keepdims=True)
    for bit_number in range(lax.axis_size("blk").bit_length() - 1):
        squares = squares + partner(squares, "blk", 1 << bit_number)

    spot = jnp.where(chip % 2 == 1, (chip + 1) // 2, (chips - chip // 2) % chips)
    shard = jnp.arange(groups * parts, dtype=jnp.int32) ^ (group * parts)
    place = (spot - 1 - shard) % chips + jnp.where(shard // chips == core, 0, chips)
    own_shard = (core * chips + spot) ^ (group * parts)
    place = jnp.concatenate([place, own_shard[None]]).astype(jnp.int32)

    unit = gate_weight.shape[1] // sum(CHUNK_UNITS)
    edges = [sum(CHUNK_UNITS[:i]) for i in range(len(CHUNK_UNITS) + 1)]
    f32 = jnp.float32
    n_chunks = len(CHUNK_UNITS)
    total = None
    chunks = [{} for _ in range(n_chunks)]
    ready = bring((gate_weight, up_weight), (READY, 2, tokens.shape[1], unit), 0, False, [tokens])
    last = [ready]

    def turn_of(k, stage):
        return k + stage - (k == 0 and stage > 0)

    flowing = [0, 2 * chips, 2 * chips - 1, chips, None, *range(chips - 1, 0, -1)]
    closing = [2 * chips, None, 2 * chips - 1]
    for turn in range(n_chunks + 2 * chips):
        if turn == n_chunks:
            shape = (READY_DOWN, 2 * unit, down_weight.shape[1])
            ready = bring((down_weight,), shape, 0, True, last)
            last = [ready]
        for stage in flowing if turn < n_chunks + chips else closing:
            if stage is None:
                for k in range(n_chunks):
                    for j in range(1, chips - 1):
                        if turn_of(k, chips + j) == turn:
                            last = last + [chunks[k]["hidden"][j]]
                if turn == 1:
                    last = last + squares
                continue
            for k in range(n_chunks):
                if turn_of(k, stage) != turn:
                    continue
                units, chunk = CHUNK_UNITS[k], chunks[k]
                is_last = k == n_chunks - 1
                if stage == 0:
                    ride = squares if k == 0 else None
                    keep, send, *rest = gate_up(
                        place, blocks, gate_weight, up_weight, ready, unit, edges[k], units, last,
                        not is_last, ride,
                    )
                    ready = rest[-1] if rest else None
                    last = [keep]
                    chunk.update(own=keep, flow=None)
                    if k == 0:
                        chunk["other"] = partner(send, "blk", 1)
                        squares = [rest[0]] + [partner(rest[0], "grp", i) for i in range(1, groups)]
                elif stage < chips:
                    flow = pass_on(
                        stage - 1, chips, chunk["own"], chunk["other"], chunk["flow"], last
                    )
                    last = [flow]
                    chunk["flow"] = along_ring(flow)
                elif stage == chips:
                    hidden = hidden_units(
                        place, chunk["flow"], chunk["own"], chunk["other"], squares, last
                    )
                    last = [hidden]
                    chunk["hidden"] = [hidden]
                    for _ in range(1, chips):
                        chunk["hidden"].append(along_ring(chunk["hidden"][-1]))
                elif stage == 2 * chips - 1:
                    ours = join(chunk["hidden"][1:] + chunk["hidden"][:1], last)
                    last = [ours]
                    chunk.update(ours=ours, theirs=partner(ours, "blk", 1))
                else:
                    total, *terms = down(
                        place, groups, chunk["ours"], chunk["theirs"], down_weight, ready, total,
                        2 * unit, edges[k] // 2, units // 2, last, is_last,
                    )
                    ready = terms[0]
                    last = [total]
        if 0 < turn < n_chunks:
            send = hold(send, last)
            last = [send]
            chunks[turn]["other"] = partner(send, "blk", 1)

    out = wide + total
    for i in range(1, groups):
        out = out + partner(terms[i - 1], "grp", i).astype(f32)
    return out


def solution(mesh):
    in_specs = (
        P("grp", "blk"),
        P("grp", None),
        P("grp", "blk", None, None),
        P("grp", "blk", None, None),
        P("grp", None),
        P("grp", None),
        P("grp"),
        P("blk"),
        P("blk", "grp"),
        P("blk", "grp"),
        P("grp", "blk"),
    )
    out_specs = P("grp", "blk")
    return jax.shard_map(
        on_device, mesh=mesh, in_specs=in_specs, out_specs=out_specs, check_vma=False
    )
```

```python
import functools
import math

import jax
import jax.numpy as jnp
from jax import lax
from jax.experimental import pallas as pl
from jax.experimental.pallas import tpu as pltpu
from jax.sharding import PartitionSpec as P

D = 16384
HEADS = 128
KV_HEADS = 8
CHUNK_UNITS = (14, 12)
SLOTS = 4
READY = 2
READY_DOWN = 1
VMEM = 38 * 1024 * 1024
SMALL_VMEM = 8 * 1024 * 1024


def partner(x, axis, distance):
    return lax.ppermute(x, axis, [(i, i ^ distance) for i in range(lax.axis_size(axis))])


def along_ring(x):
    chips = lax.axis_size("blk") // 2
    ring = [0, *range(1, chips, 2), *range(chips - 2, 0, -2)]
    hops = zip(ring, ring[1:] + ring[:1])
    return lax.ppermute(x, "blk", [(2 * a + c, 2 * b + c) for a, b in hops for c in range(2)])


def stream(units, ready, copies, ahead, prepare, compute):
    ready = min(ready, units)
    streamed = units - ready

    def start(i, slot):
        for copy in copies(ready + i, slot):
            copy.start()

    for i in range(min(2, streamed)):
        start(i, i)
    prepare()
    for i in range(ready):
        compute(i, None)

    def step(i, _):
        slot = lax.rem(i, SLOTS)
        for copy in copies(ready + i, slot):
            copy.wait()

        @pl.when(i == 0)
        def _():
            for later in range(2, min(SLOTS - 1, streamed)):
                start(later, later)

        later = i + SLOTS - 1

        @pl.when(later < streamed)
        def _():
            start(later, lax.rem(later, SLOTS))

        @pl.when(i == max(streamed - SLOTS + 1, 0))
        def _():
            for copy in ahead:
                copy.start()

        compute(ready + i, slot)
        return 0

    lax.fori_loop(0, streamed, step, 0)
    for copy in ahead:
        copy.wait()


def bring_kernel(n_weights, first_unit, by_rows, *refs):
    weights, out_ref, sems = refs[:n_weights], refs[-2], refs[-1]
    copies = tiles(weights, out_ref, sems, first_unit, by_rows)
    for copy in copies:
        copy.start()
    for copy in copies:
        copy.wait()


def tiles(weights, out_ref, sems, first_unit, by_rows):
    count = out_ref.shape[0]
    unit = out_ref.shape[1] if by_rows else out_ref.shape[2] // len(weights)
    copies = []
    for i in range(count):
        here = slice((first_unit + i) * unit, (first_unit + i + 1) * unit)
        for j, weight in enumerate(weights):
            source = weight.at[here, :] if by_rows else weight.at[:, here]
            target = out_ref.at[i] if by_rows else out_ref.at[i, :, j * unit : (j + 1) * unit]
            copies.append(pltpu.make_async_copy(source, target, sems.at[i, j]))
    return copies


def bring(weights, shape, first_unit, by_rows, after):
    return pl.pallas_call(
        functools.partial(bring_kernel, len(weights), first_unit, by_rows),
        in_specs=[pl.BlockSpec(memory_space=pltpu.HBM)] * len(weights)
        + [pl.BlockSpec(memory_space=pl.ANY)] * len(after),
        out_specs=pl.BlockSpec(memory_space=pltpu.VMEM),
        out_shape=jax.ShapeDtypeStruct(shape, jnp.bfloat16),
        scratch_shapes=[pltpu.SemaphoreType.DMA((shape[0], len(weights)))],
        compiler_params=pltpu.CompilerParams(vmem_limit_bytes=VMEM),
        cost_estimate=pl.CostEstimate(
            flops=0, bytes_accessed=4 * math.prod(shape), transcendentals=0
        ),
    )(*weights, *after)


def gate_up_kernel(n_blocks, has_ride, has_next, first_unit, units, place_ref, *refs):
    blocks, (gate_ref, up_ref, ready_ref) = refs[:n_blocks], refs[n_blocks : n_blocks + 3]
    keep_ref, send_ref, *rest = refs[len(refs) - 6 - has_ride - has_next :]
    x_ref, held, sems, next_sems = rest[-4:]
    half = keep_ref.shape[1]
    unit = held.shape[2] // 2
    parts = (place_ref.shape[0] - 1) // n_blocks
    rows = blocks[0].shape[0] // parts
    ahead = []
    if has_next:
        ahead = tiles((gate_ref, up_ref), rest[has_ride], next_sems, first_unit + units, False)

    def copies(i, slot):
        columns = pl.ds(pl.multiple_of((first_unit + i) * unit, unit), unit)
        return [
            pltpu.make_async_copy(
                weight.at[:, columns], held.at[slot, :, j * unit : (j + 1) * unit], sems.at[slot, j]
            )
            for j, weight in enumerate((gate_ref, up_ref))
        ]

    def prepare():
        if has_ride:
            rest[0][...] = refs[n_blocks + 3][...]
        for i in range(n_blocks * parts):
            to = pl.ds(pl.multiple_of(place_ref[i] * rows, rows), rows)
            x_ref[to, :] = blocks[i // parts][i % parts * rows : (i % parts + 1) * rows, :]

    def compute(i, slot):
        columns = pl.ds(i * unit if slot is None else pl.multiple_of(i * unit, unit), unit)
        weights = ready_ref[i] if slot is None else held[slot]
        y = jnp.dot(x_ref[...], weights, preferred_element_type=jnp.float32)
        for j in range(2):
            here = slice(j * unit, (j + 1) * unit)
            keep_ref[j, :, columns] = y[:half, here].astype(jnp.bfloat16)
            send_ref[j, :, columns] = y[half:, here].astype(jnp.bfloat16)

    stream(units, ready_ref.shape[0], copies, ahead, prepare, compute)


def gate_up(
    place, blocks, gate_weight, up_weight, ready, unit, start, units, after, has_next, ride=None
):
    rows, depth = blocks[0].shape
    total = rows * len(blocks)
    cols = units * unit
    rides = [] if ride is None else [ride]
    vmem = pl.BlockSpec(memory_space=pltpu.VMEM)
    outs = [jax.ShapeDtypeStruct((2, total // 2, cols), jnp.bfloat16)] * 2
    outs += [jax.ShapeDtypeStruct(r.shape, r.dtype) for r in rides]
    outs += [jax.ShapeDtypeStruct(ready.shape, ready.dtype)] * has_next
    return pl.pallas_call(
        functools.partial(gate_up_kernel, len(blocks), len(rides), has_next, start, units),
        in_specs=[pl.BlockSpec(memory_space=pltpu.SMEM)]
        + [vmem] * len(blocks)
        + [pl.BlockSpec(memory_space=pltpu.HBM)] * 2
        + [vmem] * (1 + len(rides))
        + [pl.BlockSpec(memory_space=pl.ANY)] * len(after),
        out_specs=[vmem] * len(outs),
        out_shape=outs,
        scratch_shapes=[
            pltpu.VMEM((total, depth), jnp.bfloat16),
            pltpu.VMEM((SLOTS, depth, 2 * unit), jnp.bfloat16),
            pltpu.SemaphoreType.DMA((SLOTS, 2)),
            pltpu.SemaphoreType.DMA((READY, 2)),
        ],
        compiler_params=pltpu.CompilerParams(vmem_limit_bytes=VMEM),
        cost_estimate=pl.CostEstimate(
            flops=4 * total * depth * cols,
            bytes_accessed=4 * depth * cols + 2 * total * depth + 4 * total * cols,
            transcendentals=0,
        ),
    )(place, *blocks, gate_weight, up_weight, ready, *rides, *after)


def nothing(*refs):
    pass


def hold(x, after):
    anywhere = pl.BlockSpec(memory_space=pl.ANY)
    return pl.pallas_call(
        nothing,
        in_specs=[anywhere] * (1 + len(after)),
        out_specs=anywhere,
        out_shape=jax.ShapeDtypeStruct(x.shape, x.dtype),
        input_output_aliases={0: 0},
        compiler_params=pltpu.CompilerParams(vmem_limit_bytes=SMALL_VMEM),
        cost_estimate=pl.CostEstimate(flops=0, bytes_accessed=0, transcendentals=0),
    )(x, *after)


def pass_on_kernel(shard, has_flow, own_ref, other_ref, *refs):
    out_ref = refs[-1]
    rows = out_ref.shape[1]
    here = slice(shard * rows, (shard + 1) * rows)
    total = own_ref[:, here].astype(jnp.float32) + other_ref[:, here].astype(jnp.float32)
    if has_flow:
        total = total + refs[0][...].astype(jnp.float32)
    out_ref[...] = total.astype(jnp.bfloat16)


def pass_on(shard, shards, own, other, flow, after):
    vmem = pl.BlockSpec(memory_space=pltpu.VMEM)
    flows = [] if flow is None else [flow]
    return pl.pallas_call(
        functools.partial(pass_on_kernel, shard, len(flows)),
        in_specs=[vmem] * (2 + len(flows)) + [pl.BlockSpec(memory_space=pl.ANY)] * len(after),
        out_specs=vmem,
        out_shape=jax.ShapeDtypeStruct(
            (2, own.shape[1] // shards, own.shape[2]), jnp.bfloat16
        ),
        compiler_params=pltpu.CompilerParams(vmem_limit_bytes=SMALL_VMEM),
        cost_estimate=pl.CostEstimate(
            flops=2 * own.size // shards, bytes_accessed=8 * own.size // shards, transcendentals=0
        ),
    )(own, other, *flows, *after)


def hidden_kernel(n_squares, width, place_ref, flow_ref, own_ref, other_ref, *refs):
    squares, out_ref, all_ref = refs[:n_squares], refs[-2], refs[-1]
    rows = flow_ref.shape[1]
    for i, square in enumerate(squares):
        all_ref[i * square.shape[0] : (i + 1) * square.shape[0]] = square[...]
    here = pl.ds(pl.multiple_of(place_ref[place_ref.shape[0] - 1] * rows, rows), rows)
    inverse = lax.rsqrt(all_ref[here, :] / width + 1e-05)
    gate, up = [
        (
            own_ref[i, -rows:].astype(jnp.float32)
            + other_ref[i, -rows:].astype(jnp.float32)
            + flow_ref[i].astype(jnp.float32)
        )
        * inverse
        for i in range(2)
    ]
    out_ref[...] = (gate / (1 + jnp.exp(-gate)) * up).astype(jnp.bfloat16)


def hidden_units(place, flow, own, other, squares, after):
    _, rows, cols = flow.shape
    vmem = pl.BlockSpec(memory_space=pltpu.VMEM)
    return pl.pallas_call(
        functools.partial(hidden_kernel, len(squares), D),
        in_specs=[pl.BlockSpec(memory_space=pltpu.SMEM)]
        + [vmem] * (3 + len(squares))
        + [pl.BlockSpec(memory_space=pl.ANY)] * len(after),
        out_specs=vmem,
        out_shape=jax.ShapeDtypeStruct((rows, cols), jnp.bfloat16),
        scratch_shapes=[pltpu.VMEM((len(squares) * squares[0].shape[0], 1), jnp.float32)],
        compiler_params=pltpu.CompilerParams(vmem_limit_bytes=SMALL_VMEM),
        cost_estimate=pl.CostEstimate(
            flops=16 * rows * cols, bytes_accessed=14 * rows * cols, transcendentals=rows * cols
        ),
    )(place, flow, own, other, *squares, *after)


def join_kernel(n_shards, *refs):
    out_ref = refs[-1]
    rows = refs[0].shape[0]
    for i, shard in enumerate(refs[:n_shards]):
        out_ref[i * rows : (i + 1) * rows] = shard[...]


def join(shards, after):
    rows, cols = shards[0].shape
    vmem = pl.BlockSpec(memory_space=pltpu.VMEM)
    return pl.pallas_call(
        functools.partial(join_kernel, len(shards)),
        in_specs=[vmem] * len(shards) + [pl.BlockSpec(memory_space=pl.ANY)] * len(after),
        out_specs=vmem,
        out_shape=jax.ShapeDtypeStruct((rows * len(shards), cols), jnp.bfloat16),
        compiler_params=pltpu.CompilerParams(vmem_limit_bytes=SMALL_VMEM),
        cost_estimate=pl.CostEstimate(
            flops=0, bytes_accessed=4 * rows * len(shards) * cols, transcendentals=0
        ),
    )(*shards, *after)


def down_kernel(has_total, n_outs, first_unit, units, place_ref, *refs):
    ours_ref, theirs_ref, weight_ref, ready_ref = refs[:4]
    is_last = n_outs > 2
    x_ref, held, sems, next_sems, *rest = refs[len(refs) - 4 - is_last :]
    outs = refs[len(refs) - 4 - is_last - n_outs : len(refs) - 4 - is_last]
    total_ref = rest[0] if is_last else outs[0]
    half = ours_ref.shape[0]
    unit = held.shape[1]
    ahead = [] if is_last else tiles((weight_ref,), outs[1], next_sems, first_unit + units, True)

    def copies(i, slot):
        here = pl.ds(pl.multiple_of((first_unit + i) * unit, unit), unit)
        return [pltpu.make_async_copy(weight_ref.at[here, :], held.at[slot], sems.at[slot])]

    def prepare():
        x_ref[:half] = ours_ref[...]
        x_ref[half:] = theirs_ref[...]
        total_ref[...] = refs[4][...] if has_total else jnp.zeros_like(total_ref)

    def compute(i, slot):
        columns = pl.ds(i * unit if slot is None else pl.multiple_of(i * unit, unit), unit)
        weight = ready_ref[i] if slot is None else held[slot]
        total_ref[...] += jnp.dot(x_ref[:, columns], weight, preferred_element_type=jnp.float32)

    stream(units, ready_ref.shape[0], copies, ahead, prepare, compute)
    if is_last:
        parts = (place_ref.shape[0] - 1) // n_outs
        for i in range(n_outs * parts):
            out_ref = outs[i // parts]
            rows = out_ref.shape[0] // parts
            term = total_ref[pl.ds(pl.multiple_of(place_ref[i] * rows, rows), rows), :]
            out_ref[i % parts * rows : (i % parts + 1) * rows, :] = term.astype(out_ref.dtype)


def down(place, groups, ours, theirs, weight, ready, total, unit, start, units, after, is_last):
    half, cols = ours.shape
    width = weight.shape[1]
    has_total = total is not None
    vmem = pl.BlockSpec(memory_space=pltpu.VMEM)
    rows = 2 * half // groups
    outs = [
        jax.ShapeDtypeStruct((2 * half, width), jnp.float32),
        jax.ShapeDtypeStruct(ready.shape, ready.dtype),
    ]
    if is_last:
        outs = [jax.ShapeDtypeStruct((rows, width), jnp.float32)]
        outs += [jax.ShapeDtypeStruct((rows, width), jnp.bfloat16)] * (groups - 1)
    return pl.pallas_call(
        functools.partial(down_kernel, has_total, len(outs), start, units),
        in_specs=[pl.BlockSpec(memory_space=pltpu.SMEM), vmem, vmem]
        + [pl.BlockSpec(memory_space=pltpu.HBM), vmem]
        + [vmem] * has_total
        + [pl.BlockSpec(memory_space=pl.ANY)] * len(after),
        out_specs=[vmem] * len(outs),
        out_shape=outs,
        scratch_shapes=[
            pltpu.VMEM((2 * half, cols), jnp.bfloat16),
            pltpu.VMEM((SLOTS, unit, width), jnp.bfloat16),
            pltpu.SemaphoreType.DMA((SLOTS,)),
            pltpu.SemaphoreType.DMA((READY_DOWN, 1)),
        ]
        + [pltpu.VMEM((2 * half, width), jnp.float32)] * is_last,
        compiler_params=pltpu.CompilerParams(vmem_limit_bytes=VMEM),
        cost_estimate=pl.CostEstimate(
            flops=4 * half * units * unit * width,
            bytes_accessed=2 * units * unit * width + 16 * half * width,
            transcendentals=0,
        ),
    )(place, ours, theirs, weight, ready, *([total] if has_total else []), *after)


def attend(residual_in, queries, key_cache, value_cache, key_new, value_new, lengths):
    cycle_size = lax.axis_size("blk")
    quarters = cycle_size // KV_HEADS
    per_kv = HEADS // KV_HEADS
    own_heads = HEADS // cycle_size
    head_size = key_cache.shape[3]
    seq_rows = residual_in.shape[0]
    positions_here = key_cache.shape[2]
    blk_index = lax.axis_index("blk")
    kv_head = blk_index // quarters
    quarter = blk_index % quarters
    score_scale = 1.0 / math.sqrt(head_size)
    group_queries = lax.dynamic_slice_in_dim(
        queries, kv_head * per_kv * head_size, per_kv * head_size, 1
    )
    group_queries = group_queries.astype(jnp.float32).reshape(seq_rows, per_kv, head_size)
    fresh_key = lax.dynamic_slice_in_dim(key_new, kv_head * head_size, head_size, 1).astype(
        jnp.float32
    )
    fresh_value = lax.dynamic_slice_in_dim(value_new, kv_head * head_size, head_size, 1).astype(
        jnp.float32
    )
    keys_here = key_cache[:, 0].astype(jnp.float32)
    values_here = value_cache[:, 0].astype(jnp.float32)
    scores = jnp.einsum("shd,spd->shp", group_queries, keys_here) * score_scale
    fresh_scores = jnp.einsum("shd,sd->sh", group_queries, fresh_key) * score_scale
    places = quarter * positions_here + jnp.arange(positions_here, dtype=jnp.int32)
    usable = (places[None, :] < lengths[:, None])[:, None, :]
    with_fresh = quarter == 0
    largest = jnp.maximum(
        jnp.max(jnp.where(usable, scores, -1e30), axis=2),
        jnp.where(with_fresh, fresh_scores, -1e30),
    )
    weights = jnp.where(usable, jnp.exp(scores - largest[..., None]), 0.0)
    fresh_weight = jnp.where(with_fresh, jnp.exp(fresh_scores - largest), 0.0)
    totals = jnp.sum(weights, axis=2) + fresh_weight
    weighted = (
        jnp.einsum("shp,spd->shd", weights, values_here)
        + fresh_weight[..., None] * fresh_value[:, None, :]
    )
    for bit_number in range(quarters.bit_length() - 1):
        peer_max, peer_total, peer_weighted = partner(
            (largest, totals, weighted), "blk", 1 << bit_number
        )
        merged = jnp.maximum(largest, peer_max)
        mine_factor = jnp.exp(largest - merged)
        peer_factor = jnp.exp(peer_max - merged)
        totals = totals * mine_factor + peer_total * peer_factor
        weighted = weighted * mine_factor[..., None] + peer_weighted * peer_factor[..., None]
        largest = merged
    attention = weighted / totals[..., None]
    own_output = lax.dynamic_slice_in_dim(attention, quarter * own_heads, own_heads, 1).reshape(
        seq_rows, own_heads * head_size
    )
    return residual_in.astype(jnp.float32) + own_output


def on_device(
    residual_in,
    queries,
    key_cache,
    value_cache,
    key_new,
    value_new,
    lengths,
    ffn_gain,
    gate_weight,
    up_weight,
    down_weight,
):
    groups = lax.axis_size("grp")
    group = lax.axis_index("grp")
    chips = lax.axis_size("blk") // 2
    chip, core = lax.axis_index("blk") // 2, lax.axis_index("blk") % 2
    rows = residual_in.shape[0]
    parts = 2 * chips // groups

    wide = attend(residual_in, queries, key_cache, value_cache, key_new, value_new, lengths)

    tokens = (wide * ffn_gain.astype(jnp.float32)[None, :]).astype(jnp.bfloat16)
    blocks = [tokens] + [partner(tokens, "grp", i) for i in range(1, groups)]

    squares = jnp.sum(wide * wide, axis=1, keepdims=True)
    for bit_number in range(lax.axis_size("blk").bit_length() - 1):
        squares = squares + partner(squares, "blk", 1 << bit_number)

    spot = jnp.where(chip % 2 == 1, (chip + 1) // 2, (chips - chip // 2) % chips)
    shard = jnp.arange(groups * parts, dtype=jnp.int32) ^ (group * parts)
    place = (spot - 1 - shard) % chips + jnp.where(shard // chips == core, 0, chips)
    own_shard = (core * chips + spot) ^ (group * parts)
    place = jnp.concatenate([place, own_shard[None]]).astype(jnp.int32)

    unit = gate_weight.shape[1] // sum(CHUNK_UNITS)
    edges = [sum(CHUNK_UNITS[:i]) for i in range(len(CHUNK_UNITS) + 1)]
    f32 = jnp.float32
    n_chunks = len(CHUNK_UNITS)
    total = None
    chunks = [{} for _ in range(n_chunks)]
    shape = (READY, tokens.shape[1], 2 * unit)
    ready = bring((gate_weight, up_weight), shape, 0, False, [tokens])
    last = [ready]

    def turn_of(k, stage):
        return k + stage - (k == 0 and stage > 0)

    flowing = [0, 2 * chips, chips, None, *range(chips - 1, 0, -1), 2 * chips - 1]
    closing = [2 * chips, 2 * chips - 1, None]
    for turn in range(n_chunks + 2 * chips):
        if turn == n_chunks:
            shape = (READY_DOWN, 2 * unit, down_weight.shape[1])
            ready = bring((down_weight,), shape, 0, True, last)
            last = [ready]
        for stage in flowing if turn < n_chunks + chips else closing:
            if stage is None:
                for k in range(n_chunks):
                    for j in range(1, chips - 1):
                        if turn_of(k, chips + j) == turn:
                            last = last + [chunks[k]["hidden"][j]]
                if turn == 1:
                    last = last + squares
                continue
            for k in range(n_chunks):
                if turn_of(k, stage) != turn:
                    continue
                units, chunk = CHUNK_UNITS[k], chunks[k]
                is_last = k == n_chunks - 1
                if stage == 0:
                    ride = squares if k == 0 else None
                    keep, send, *rest = gate_up(
                        place, blocks, gate_weight, up_weight, ready, unit, edges[k], units, last,
                        not is_last, ride,
                    )
                    ready = rest[-1] if rest else None
                    last = [keep]
                    chunk.update(own=keep, flow=None)
                    if k == 0:
                        chunk["other"] = partner(send, "blk", 1)
                        squares = [rest[0]] + [partner(rest[0], "grp", i) for i in range(1, groups)]
                elif stage < chips:
                    flow = pass_on(
                        stage - 1, chips, chunk["own"], chunk["other"], chunk["flow"], last
                    )
                    last = [flow]
                    chunk["flow"] = along_ring(flow)
                elif stage == chips:
                    hidden = hidden_units(
                        place, chunk["flow"], chunk["own"], chunk["other"], squares, last
                    )
                    last = [hidden]
                    chunk["hidden"] = [hidden]
                    for _ in range(1, chips):
                        chunk["hidden"].append(along_ring(chunk["hidden"][-1]))
                elif stage == 2 * chips - 1:
                    ours = join(chunk["hidden"][1:] + chunk["hidden"][:1], last)
                    last = [ours]
                    chunk.update(ours=ours, theirs=partner(ours, "blk", 1))
                else:
                    total, *terms = down(
                        place, groups, chunk["ours"], chunk["theirs"], down_weight, ready, total,
                        2 * unit, edges[k] // 2, units // 2, last, is_last,
                    )
                    ready = terms[0]
                    last = [total]
        if 0 < turn < n_chunks:
            send = hold(send, last)
            last = [send]
            chunks[turn]["other"] = partner(send, "blk", 1)

    out = wide + total
    for i in range(1, groups):
        out = out + partner(terms[i - 1], "grp", i).astype(f32)
    return out


def solution(mesh):
    in_specs = (
        P("grp", "blk"),
        P("grp", None),
        P("grp", "blk", None, None),
        P("grp", "blk", None, None),
        P("grp", None),
        P("grp", None),
        P("grp"),
        P("blk"),
        P("blk", "grp"),
        P("blk", "grp"),
        P("grp", "blk"),
    )
    out_specs = P("grp", "blk")
    return jax.shard_map(
        on_device, mesh=mesh, in_specs=in_specs, out_specs=out_specs, check_vma=False
    )
```

```python
import functools
import math

import jax
import jax.numpy as jnp
from jax import lax
from jax.experimental import pallas as pl
from jax.experimental.pallas import tpu as pltpu
from jax.sharding import PartitionSpec as P

D = 16384
HEADS = 128
KV_HEADS = 8
CHUNK_UNITS = (14, 12)
SLOTS = 4
READY = 2
READY_DOWN = 1
VMEM = 38 * 1024 * 1024
SMALL_VMEM = 8 * 1024 * 1024


def partner(x, axis, distance):
    return lax.ppermute(x, axis, [(i, i ^ distance) for i in range(lax.axis_size(axis))])


def along_ring(x):
    chips = lax.axis_size("blk") // 2
    ring = [0, *range(1, chips, 2), *range(chips - 2, 0, -2)]
    hops = zip(ring, ring[1:] + ring[:1])
    return lax.ppermute(x, "blk", [(2 * a + c, 2 * b + c) for a, b in hops for c in range(2)])


def stream(units, ready, copies, ahead, prepare, compute):
    ready = min(ready, units)
    streamed = units - ready

    def start(i, slot):
        for copy in copies(ready + i, slot):
            copy.start()

    for i in range(min(2, streamed)):
        start(i, i)
    prepare()
    for i in range(ready):
        compute(i, None)

    def step(i, _):
        slot = lax.rem(i, SLOTS)
        for copy in copies(ready + i, slot):
            copy.wait()

        @pl.when(i == 0)
        def _():
            for later in range(2, min(SLOTS - 1, streamed)):
                start(later, later)

        later = i + SLOTS - 1

        @pl.when(later < streamed)
        def _():
            start(later, lax.rem(later, SLOTS))

        @pl.when(i == max(streamed - SLOTS + 1, 0))
        def _():
            for copy in ahead:
                copy.start()

        compute(ready + i, slot)
        return 0

    lax.fori_loop(0, streamed, step, 0)
    for copy in ahead:
        copy.wait()


def bring_kernel(n_weights, first_unit, by_rows, *refs):
    weights, out_ref, sems = refs[:n_weights], refs[-2], refs[-1]
    copies = tiles(weights, out_ref, sems, first_unit, by_rows)
    for copy in copies:
        copy.start()
    for copy in copies:
        copy.wait()


def tiles(weights, out_ref, sems, first_unit, by_rows):
    count = out_ref.shape[0]
    unit = out_ref.shape[1] if by_rows else out_ref.shape[2] // len(weights)
    copies = []
    for i in range(count):
        here = slice((first_unit + i) * unit, (first_unit + i + 1) * unit)
        for j, weight in enumerate(weights):
            source = weight.at[here, :] if by_rows else weight.at[:, here]
            target = out_ref.at[i] if by_rows else out_ref.at[i, :, j * unit : (j + 1) * unit]
            copies.append(pltpu.make_async_copy(source, target, sems.at[i, j]))
    return copies


def bring(weights, shape, first_unit, by_rows, after):
    return pl.pallas_call(
        functools.partial(bring_kernel, len(weights), first_unit, by_rows),
        in_specs=[pl.BlockSpec(memory_space=pltpu.HBM)] * len(weights)
        + [pl.BlockSpec(memory_space=pl.ANY)] * len(after),
        out_specs=pl.BlockSpec(memory_space=pltpu.VMEM),
        out_shape=jax.ShapeDtypeStruct(shape, jnp.bfloat16),
        scratch_shapes=[pltpu.SemaphoreType.DMA((shape[0], len(weights)))],
        compiler_params=pltpu.CompilerParams(vmem_limit_bytes=VMEM),
        cost_estimate=pl.CostEstimate(
            flops=0, bytes_accessed=4 * math.prod(shape), transcendentals=0
        ),
    )(*weights, *after)


def gate_up_kernel(n_blocks, has_next, first_unit, units, place_ref, *refs):
    blocks, (gate_ref, up_ref, ready_ref) = refs[:n_blocks], refs[n_blocks : n_blocks + 3]
    keep_ref, send_ref, *rest = refs[len(refs) - 6 - has_next :]
    x_ref, held, sems, next_sems = rest[-4:]
    half = keep_ref.shape[1]
    unit = held.shape[2] // 2
    parts = (place_ref.shape[0] - 1) // n_blocks
    rows = blocks[0].shape[0] // parts
    ahead = []
    if has_next:
        ahead = tiles((gate_ref, up_ref), rest[0], next_sems, first_unit + units, False)

    def copies(i, slot):
        columns = pl.ds(pl.multiple_of((first_unit + i) * unit, unit), unit)
        return [
            pltpu.make_async_copy(
                weight.at[:, columns], held.at[slot, :, j * unit : (j + 1) * unit], sems.at[slot, j]
            )
            for j, weight in enumerate((gate_ref, up_ref))
        ]

    def prepare():
        for i in range(n_blocks * parts):
            to = pl.ds(pl.multiple_of(place_ref[i] * rows, rows), rows)
            x_ref[to, :] = blocks[i // parts][i % parts * rows : (i % parts + 1) * rows, :]

    def compute(i, slot):
        columns = pl.ds(i * unit if slot is None else pl.multiple_of(i * unit, unit), unit)
        weights = ready_ref[i] if slot is None else held[slot]
        y = jnp.dot(x_ref[...], weights, preferred_element_type=jnp.float32)
        for j in range(2):
            here = slice(j * unit, (j + 1) * unit)
            keep_ref[j, :, columns] = y[:half, here].astype(jnp.bfloat16)
            send_ref[j, :, columns] = y[half:, here].astype(jnp.bfloat16)

    stream(units, ready_ref.shape[0], copies, ahead, prepare, compute)


def gate_up(
    place, blocks, gate_weight, up_weight, ready, unit, start, units, after, has_next
):
    rows, depth = blocks[0].shape
    total = rows * len(blocks)
    cols = units * unit
    vmem = pl.BlockSpec(memory_space=pltpu.VMEM)
    outs = [jax.ShapeDtypeStruct((2, total // 2, cols), jnp.bfloat16)] * 2
    outs += [jax.ShapeDtypeStruct(ready.shape, ready.dtype)] * has_next
    return pl.pallas_call(
        functools.partial(gate_up_kernel, len(blocks), has_next, start, units),
        in_specs=[pl.BlockSpec(memory_space=pltpu.SMEM)]
        + [vmem] * len(blocks)
        + [pl.BlockSpec(memory_space=pltpu.HBM)] * 2
        + [vmem]
        + [pl.BlockSpec(memory_space=pl.ANY)] * len(after),
        out_specs=[vmem] * len(outs),
        out_shape=outs,
        scratch_shapes=[
            pltpu.VMEM((total, depth), jnp.bfloat16),
            pltpu.VMEM((SLOTS, depth, 2 * unit), jnp.bfloat16),
            pltpu.SemaphoreType.DMA((SLOTS, 2)),
            pltpu.SemaphoreType.DMA((READY, 2)),
        ],
        compiler_params=pltpu.CompilerParams(vmem_limit_bytes=VMEM),
        cost_estimate=pl.CostEstimate(
            flops=4 * total * depth * cols,
            bytes_accessed=4 * depth * cols + 2 * total * depth + 4 * total * cols,
            transcendentals=0,
        ),
    )(place, *blocks, gate_weight, up_weight, ready, *after)


def nothing(*refs):
    pass


def hold(x, after):
    anywhere = pl.BlockSpec(memory_space=pl.ANY)
    return pl.pallas_call(
        nothing,
        in_specs=[anywhere] * (1 + len(after)),
        out_specs=anywhere,
        out_shape=jax.ShapeDtypeStruct(x.shape, x.dtype),
        input_output_aliases={0: 0},
        compiler_params=pltpu.CompilerParams(vmem_limit_bytes=SMALL_VMEM),
        cost_estimate=pl.CostEstimate(flops=0, bytes_accessed=0, transcendentals=0),
    )(x, *after)


def pass_on_kernel(shard, has_flow, own_ref, other_ref, *refs):
    out_ref = refs[-1]
    rows = out_ref.shape[1]
    here = slice(shard * rows, (shard + 1) * rows)
    total = own_ref[:, here].astype(jnp.float32) + other_ref[:, here].astype(jnp.float32)
    if has_flow:
        total = total + refs[0][...].astype(jnp.float32)
    out_ref[...] = total.astype(jnp.bfloat16)


def pass_on(shard, shards, own, other, flow, after):
    vmem = pl.BlockSpec(memory_space=pltpu.VMEM)
    flows = [] if flow is None else [flow]
    return pl.pallas_call(
        functools.partial(pass_on_kernel, shard, len(flows)),
        in_specs=[vmem] * (2 + len(flows)) + [pl.BlockSpec(memory_space=pl.ANY)] * len(after),
        out_specs=vmem,
        out_shape=jax.ShapeDtypeStruct(
            (2, own.shape[1] // shards, own.shape[2]), jnp.bfloat16
        ),
        compiler_params=pltpu.CompilerParams(vmem_limit_bytes=SMALL_VMEM),
        cost_estimate=pl.CostEstimate(
            flops=2 * own.size // shards, bytes_accessed=8 * own.size // shards, transcendentals=0
        ),
    )(own, other, *flows, *after)


def hidden_kernel(n_squares, width, place_ref, flow_ref, own_ref, other_ref, *refs):
    squares, out_ref, all_ref = refs[:n_squares], refs[-2], refs[-1]
    rows = flow_ref.shape[1]
    for i, square in enumerate(squares):
        all_ref[i * square.shape[0] : (i + 1) * square.shape[0]] = square[...]
    here = pl.ds(pl.multiple_of(place_ref[place_ref.shape[0] - 1] * rows, rows), rows)
    inverse = lax.rsqrt(all_ref[here, :] / width + 1e-05)
    gate, up = [
        (
            own_ref[i, -rows:].astype(jnp.float32)
            + other_ref[i, -rows:].astype(jnp.float32)
            + flow_ref[i].astype(jnp.float32)
        )
        * inverse
        for i in range(2)
    ]
    out_ref[...] = (gate / (1 + jnp.exp(-gate)) * up).astype(jnp.bfloat16)


def hidden_units(place, flow, own, other, squares, after):
    _, rows, cols = flow.shape
    vmem = pl.BlockSpec(memory_space=pltpu.VMEM)
    return pl.pallas_call(
        functools.partial(hidden_kernel, len(squares), D),
        in_specs=[pl.BlockSpec(memory_space=pltpu.SMEM)]
        + [vmem] * (3 + len(squares))
        + [pl.BlockSpec(memory_space=pl.ANY)] * len(after),
        out_specs=vmem,
        out_shape=jax.ShapeDtypeStruct((rows, cols), jnp.bfloat16),
        scratch_shapes=[pltpu.VMEM((len(squares) * squares[0].shape[0], 1), jnp.float32)],
        compiler_params=pltpu.CompilerParams(vmem_limit_bytes=SMALL_VMEM),
        cost_estimate=pl.CostEstimate(
            flops=16 * rows * cols, bytes_accessed=14 * rows * cols, transcendentals=rows * cols
        ),
    )(place, flow, own, other, *squares, *after)


def join_kernel(n_shards, *refs):
    out_ref = refs[-1]
    rows = refs[0].shape[0]
    for i, shard in enumerate(refs[:n_shards]):
        out_ref[i * rows : (i + 1) * rows] = shard[...]


def join(shards, after):
    rows, cols = shards[0].shape
    vmem = pl.BlockSpec(memory_space=pltpu.VMEM)
    return pl.pallas_call(
        functools.partial(join_kernel, len(shards)),
        in_specs=[vmem] * len(shards) + [pl.BlockSpec(memory_space=pl.ANY)] * len(after),
        out_specs=vmem,
        out_shape=jax.ShapeDtypeStruct((rows * len(shards), cols), jnp.bfloat16),
        compiler_params=pltpu.CompilerParams(vmem_limit_bytes=SMALL_VMEM),
        cost_estimate=pl.CostEstimate(
            flops=0, bytes_accessed=4 * rows * len(shards) * cols, transcendentals=0
        ),
    )(*shards, *after)


def down_kernel(has_total, n_outs, first_unit, units, place_ref, *refs):
    ours_ref, theirs_ref, weight_ref, ready_ref = refs[:4]
    is_last = n_outs > 2
    x_ref, held, sems, next_sems, *rest = refs[len(refs) - 4 - is_last :]
    outs = refs[len(refs) - 4 - is_last - n_outs : len(refs) - 4 - is_last]
    total_ref = rest[0] if is_last else outs[0]
    half = ours_ref.shape[0]
    unit = held.shape[1]
    ahead = [] if is_last else tiles((weight_ref,), outs[1], next_sems, first_unit + units, True)

    def copies(i, slot):
        here = pl.ds(pl.multiple_of((first_unit + i) * unit, unit), unit)
        return [pltpu.make_async_copy(weight_ref.at[here, :], held.at[slot], sems.at[slot])]

    def prepare():
        x_ref[:half] = ours_ref[...]
        x_ref[half:] = theirs_ref[...]
        total_ref[...] = refs[4][...] if has_total else jnp.zeros_like(total_ref)

    def compute(i, slot):
        columns = pl.ds(i * unit if slot is None else pl.multiple_of(i * unit, unit), unit)
        weight = ready_ref[i] if slot is None else held[slot]
        total_ref[...] += jnp.dot(x_ref[:, columns], weight, preferred_element_type=jnp.float32)

    stream(units, ready_ref.shape[0], copies, ahead, prepare, compute)
    if is_last:
        parts = (place_ref.shape[0] - 1) // n_outs
        for i in range(n_outs * parts):
            out_ref = outs[i // parts]
            rows = out_ref.shape[0] // parts
            term = total_ref[pl.ds(pl.multiple_of(place_ref[i] * rows, rows), rows), :]
            out_ref[i % parts * rows : (i % parts + 1) * rows, :] = term.astype(out_ref.dtype)


def down(place, groups, ours, theirs, weight, ready, total, unit, start, units, after, is_last):
    half, cols = ours.shape
    width = weight.shape[1]
    has_total = total is not None
    vmem = pl.BlockSpec(memory_space=pltpu.VMEM)
    rows = 2 * half // groups
    outs = [
        jax.ShapeDtypeStruct((2 * half, width), jnp.float32),
        jax.ShapeDtypeStruct(ready.shape, ready.dtype),
    ]
    if is_last:
        outs = [jax.ShapeDtypeStruct((rows, width), jnp.float32)]
        outs += [jax.ShapeDtypeStruct((rows, width), jnp.bfloat16)] * (groups - 1)
    return pl.pallas_call(
        functools.partial(down_kernel, has_total, len(outs), start, units),
        in_specs=[pl.BlockSpec(memory_space=pltpu.SMEM), vmem, vmem]
        + [pl.BlockSpec(memory_space=pltpu.HBM), vmem]
        + [vmem] * has_total
        + [pl.BlockSpec(memory_space=pl.ANY)] * len(after),
        out_specs=[vmem] * len(outs),
        out_shape=outs,
        scratch_shapes=[
            pltpu.VMEM((2 * half, cols), jnp.bfloat16),
            pltpu.VMEM((SLOTS, unit, width), jnp.bfloat16),
            pltpu.SemaphoreType.DMA((SLOTS,)),
            pltpu.SemaphoreType.DMA((READY_DOWN, 1)),
        ]
        + [pltpu.VMEM((2 * half, width), jnp.float32)] * is_last,
        compiler_params=pltpu.CompilerParams(vmem_limit_bytes=VMEM),
        cost_estimate=pl.CostEstimate(
            flops=4 * half * units * unit * width,
            bytes_accessed=2 * units * unit * width + 16 * half * width,
            transcendentals=0,
        ),
    )(place, ours, theirs, weight, ready, *([total] if has_total else []), *after)


def attend(residual_in, queries, key_cache, value_cache, key_new, value_new, lengths):
    cycle_size = lax.axis_size("blk")
    quarters = cycle_size // KV_HEADS
    per_kv = HEADS // KV_HEADS
    own_heads = HEADS // cycle_size
    head_size = key_cache.shape[3]
    seq_rows = residual_in.shape[0]
    positions_here = key_cache.shape[2]
    blk_index = lax.axis_index("blk")
    kv_head = blk_index // quarters
    quarter = blk_index % quarters
    score_scale = 1.0 / math.sqrt(head_size)
    group_queries = lax.dynamic_slice_in_dim(
        queries, kv_head * per_kv * head_size, per_kv * head_size, 1
    )
    group_queries = group_queries.astype(jnp.float32).reshape(seq_rows, per_kv, head_size)
    fresh_key = lax.dynamic_slice_in_dim(key_new, kv_head * head_size, head_size, 1).astype(
        jnp.float32
    )
    fresh_value = lax.dynamic_slice_in_dim(value_new, kv_head * head_size, head_size, 1).astype(
        jnp.float32
    )
    keys_here = key_cache[:, 0].astype(jnp.float32)
    values_here = value_cache[:, 0].astype(jnp.float32)
    scores = jnp.einsum("shd,spd->shp", group_queries, keys_here) * score_scale
    fresh_scores = jnp.einsum("shd,sd->sh", group_queries, fresh_key) * score_scale
    places = quarter * positions_here + jnp.arange(positions_here, dtype=jnp.int32)
    usable = (places[None, :] < lengths[:, None])[:, None, :]
    with_fresh = quarter == 0
    largest = jnp.maximum(
        jnp.max(jnp.where(usable, scores, -1e30), axis=2),
        jnp.where(with_fresh, fresh_scores, -1e30),
    )
    weights = jnp.where(usable, jnp.exp(scores - largest[..., None]), 0.0)
    fresh_weight = jnp.where(with_fresh, jnp.exp(fresh_scores - largest), 0.0)
    totals = jnp.sum(weights, axis=2) + fresh_weight
    weighted = (
        jnp.einsum("shp,spd->shd", weights, values_here)
        + fresh_weight[..., None] * fresh_value[:, None, :]
    )
    for bit_number in range(quarters.bit_length() - 1):
        peer_max, peer_total, peer_weighted = partner(
            (largest, totals, weighted), "blk", 1 << bit_number
        )
        merged = jnp.maximum(largest, peer_max)
        mine_factor = jnp.exp(largest - merged)
        peer_factor = jnp.exp(peer_max - merged)
        totals = totals * mine_factor + peer_total * peer_factor
        weighted = weighted * mine_factor[..., None] + peer_weighted * peer_factor[..., None]
        largest = merged
    attention = weighted / totals[..., None]
    own_output = lax.dynamic_slice_in_dim(attention, quarter * own_heads, own_heads, 1).reshape(
        seq_rows, own_heads * head_size
    )
    return residual_in.astype(jnp.float32) + own_output


def on_device(
    residual_in,
    queries,
    key_cache,
    value_cache,
    key_new,
    value_new,
    lengths,
    ffn_gain,
    gate_weight,
    up_weight,
    down_weight,
):
    groups = lax.axis_size("grp")
    group = lax.axis_index("grp")
    chips = lax.axis_size("blk") // 2
    chip, core = lax.axis_index("blk") // 2, lax.axis_index("blk") % 2
    rows = residual_in.shape[0]
    parts = 2 * chips // groups

    wide = attend(residual_in, queries, key_cache, value_cache, key_new, value_new, lengths)

    tokens = (wide * ffn_gain.astype(jnp.float32)[None, :]).astype(jnp.bfloat16)
    blocks = [tokens] + [partner(tokens, "grp", i) for i in range(1, groups)]

    squares = jnp.sum(wide * wide, axis=1, keepdims=True)
    for bit_number in range(lax.axis_size("blk").bit_length() - 1):
        squares = squares + partner(squares, "blk", 1 << bit_number)

    squares = [squares] + [partner(squares, "grp", i) for i in range(1, groups)]

    spot = jnp.where(chip % 2 == 1, (chip + 1) // 2, (chips - chip // 2) % chips)
    shard = jnp.arange(groups * parts, dtype=jnp.int32) ^ (group * parts)
    place = (spot - 1 - shard) % chips + jnp.where(shard // chips == core, 0, chips)
    own_shard = (core * chips + spot) ^ (group * parts)
    place = jnp.concatenate([place, own_shard[None]]).astype(jnp.int32)

    unit = gate_weight.shape[1] // sum(CHUNK_UNITS)
    edges = [sum(CHUNK_UNITS[:i]) for i in range(len(CHUNK_UNITS) + 1)]
    f32 = jnp.float32
    n_chunks = len(CHUNK_UNITS)
    total = None
    chunks = [{} for _ in range(n_chunks)]
    shape = (READY, tokens.shape[1], 2 * unit)
    ready = bring((gate_weight, up_weight), shape, 0, False, [tokens])
    last = [ready, *squares]

    def turn_of(k, stage):
        return k + stage - (k == 0 and stage > 0)

    flowing = [0, 2 * chips, *range(1, chips + 1), None, 2 * chips - 1]
    closing = [2 * chips, 2 * chips - 1, None]
    for turn in range(n_chunks + 2 * chips):
        if turn == n_chunks + 1:
            shape = (READY_DOWN, 2 * unit, down_weight.shape[1])
            ready = bring((down_weight,), shape, 0, True, last)
            last = [ready]
        for stage in flowing if turn < n_chunks + chips else closing:
            if stage is None:
                for k in range(n_chunks):
                    for j in range(1, chips - 1):
                        if turn_of(k, chips + j) == turn:
                            last = last + [chunks[k]["hidden"][j]]
                continue
            for k in range(n_chunks):
                if turn_of(k, stage) != turn:
                    continue
                units, chunk = CHUNK_UNITS[k], chunks[k]
                is_last = k == n_chunks - 1
                if stage == 0:
                    keep, send, *rest = gate_up(
                        place, blocks, gate_weight, up_weight, ready, unit, edges[k], units, last,
                        not is_last,
                    )
                    ready = rest[-1] if rest else None
                    last = [keep]
                    chunk.update(own=keep, flow=None)
                    if k == 0:
                        chunk["other"] = partner(send, "blk", 1)
                elif stage < chips:
                    flow = pass_on(
                        stage - 1, chips, chunk["own"], chunk["other"], chunk["flow"], last
                    )
                    last = [flow]
                    chunk["flow"] = along_ring(flow)
                elif stage == chips:
                    hidden = hidden_units(
                        place, chunk["flow"], chunk["own"], chunk["other"], squares, last
                    )
                    last = [hidden]
                    chunk["hidden"] = [hidden]
                    for _ in range(1, chips):
                        chunk["hidden"].append(along_ring(chunk["hidden"][-1]))
                elif stage == 2 * chips - 1:
                    ours = join(chunk["hidden"][1:] + chunk["hidden"][:1], last)
                    last = [ours]
                    chunk.update(ours=ours, theirs=partner(ours, "blk", 1))
                else:
                    total, *terms = down(
                        place, groups, chunk["ours"], chunk["theirs"], down_weight, ready, total,
                        2 * unit, edges[k] // 2, units // 2, last, is_last,
                    )
                    ready = terms[0]
                    last = [total]
        if 0 < turn < n_chunks:
            send = hold(send, last)
            last = [send]
            chunks[turn]["other"] = partner(send, "blk", 1)

    out = wide + total
    for i in range(1, groups):
        out = out + partner(terms[i - 1], "grp", i).astype(f32)
    return out


def solution(mesh):
    in_specs = (
        P("grp", "blk"),
        P("grp", None),
        P("grp", "blk", None, None),
        P("grp", "blk", None, None),
        P("grp", None),
        P("grp", None),
        P("grp"),
        P("blk"),
        P("blk", "grp"),
        P("blk", "grp"),
        P("grp", "blk"),
    )
    out_specs = P("grp", "blk")
    return jax.shard_map(
        on_device, mesh=mesh, in_specs=in_specs, out_specs=out_specs, check_vma=False
    )
```

```python
import functools
import math

import jax
import jax.numpy as jnp
from jax import lax
from jax.experimental import pallas as pl
from jax.experimental.pallas import tpu as pltpu
from jax.sharding import PartitionSpec as P

D = 16384
HEADS = 128
KV_HEADS = 8
CHUNK_UNITS = (14, 12)
SLOTS = 4
READY = 2
READY_DOWN = 1
VMEM = 38 * 1024 * 1024
SMALL_VMEM = 8 * 1024 * 1024


def partner(x, axis, distance):
    return lax.ppermute(x, axis, [(i, i ^ distance) for i in range(lax.axis_size(axis))])


def along_ring(x):
    chips = lax.axis_size("blk") // 2
    ring = [0, *range(1, chips, 2), *range(chips - 2, 0, -2)]
    hops = zip(ring, ring[1:] + ring[:1])
    return lax.ppermute(x, "blk", [(2 * a + c, 2 * b + c) for a, b in hops for c in range(2)])


def stream(units, ready, copies, ahead, prepare, compute):
    ready = min(ready, units)
    streamed = units - ready

    def start(i, slot):
        for copy in copies(ready + i, slot):
            copy.start()

    for i in range(min(2, streamed)):
        start(i, i)
    prepare()
    for i in range(ready):
        compute(i, None)

    def step(i, _):
        slot = lax.rem(i, SLOTS)
        for copy in copies(ready + i, slot):
            copy.wait()

        @pl.when(i == 0)
        def _():
            for later in range(2, min(SLOTS - 1, streamed)):
                start(later, later)

        later = i + SLOTS - 1

        @pl.when(later < streamed)
        def _():
            start(later, lax.rem(later, SLOTS))

        @pl.when(i == max(streamed - SLOTS + 1, 0))
        def _():
            for copy in ahead:
                copy.start()

        compute(ready + i, slot)
        return 0

    lax.fori_loop(0, streamed, step, 0)
    for copy in ahead:
        copy.wait()


def bring_kernel(n_weights, first_unit, by_rows, *refs):
    weights, out_ref, sems = refs[:n_weights], refs[-2], refs[-1]
    copies = tiles(weights, out_ref, sems, first_unit, by_rows)
    for copy in copies:
        copy.start()
    for copy in copies:
        copy.wait()


def tiles(weights, out_ref, sems, first_unit, by_rows):
    count = out_ref.shape[0]
    unit = out_ref.shape[1] if by_rows else out_ref.shape[2] // len(weights)
    copies = []
    for i in range(count):
        here = slice((first_unit + i) * unit, (first_unit + i + 1) * unit)
        for j, weight in enumerate(weights):
            source = weight.at[here, :] if by_rows else weight.at[:, here]
            target = out_ref.at[i] if by_rows else out_ref.at[i, :, j * unit : (j + 1) * unit]
            copies.append(pltpu.make_async_copy(source, target, sems.at[i, j]))
    return copies


def bring(weights, shape, first_unit, by_rows, after):
    return pl.pallas_call(
        functools.partial(bring_kernel, len(weights), first_unit, by_rows),
        in_specs=[pl.BlockSpec(memory_space=pltpu.HBM)] * len(weights)
        + [pl.BlockSpec(memory_space=pl.ANY)] * len(after),
        out_specs=pl.BlockSpec(memory_space=pltpu.VMEM),
        out_shape=jax.ShapeDtypeStruct(shape, jnp.bfloat16),
        scratch_shapes=[pltpu.SemaphoreType.DMA((shape[0], len(weights)))],
        compiler_params=pltpu.CompilerParams(vmem_limit_bytes=VMEM),
        cost_estimate=pl.CostEstimate(
            flops=0, bytes_accessed=4 * math.prod(shape), transcendentals=0
        ),
    )(*weights, *after)


def gate_up_kernel(n_blocks, has_ride, has_next, first_unit, units, place_ref, *refs):
    blocks, (gate_ref, up_ref, ready_ref) = refs[:n_blocks], refs[n_blocks : n_blocks + 3]
    keep_ref, send_ref, *rest = refs[len(refs) - 6 - has_ride - has_next :]
    x_ref, held, sems, next_sems = rest[-4:]
    half = keep_ref.shape[1]
    unit = held.shape[2] // 2
    parts = (place_ref.shape[0] - 1) // n_blocks
    rows = blocks[0].shape[0] // parts
    ahead = []
    if has_next:
        ahead = tiles((gate_ref, up_ref), rest[has_ride], next_sems, first_unit + units, False)

    def copies(i, slot):
        columns = pl.ds(pl.multiple_of((first_unit + i) * unit, unit), unit)
        return [
            pltpu.make_async_copy(
                weight.at[:, columns], held.at[slot, :, j * unit : (j + 1) * unit], sems.at[slot, j]
            )
            for j, weight in enumerate((gate_ref, up_ref))
        ]

    def prepare():
        if has_ride:
            rest[0][...] = refs[n_blocks + 3][...]
        for i in range(n_blocks * parts):
            to = pl.ds(pl.multiple_of(place_ref[i] * rows, rows), rows)
            x_ref[to, :] = blocks[i // parts][i % parts * rows : (i % parts + 1) * rows, :]

    def compute(i, slot):
        columns = pl.ds(i * unit if slot is None else pl.multiple_of(i * unit, unit), unit)
        weights = ready_ref[i] if slot is None else held[slot]
        y = jnp.dot(x_ref[...], weights, preferred_element_type=jnp.float32)
        for j in range(2):
            here = slice(j * unit, (j + 1) * unit)
            keep_ref[j, :, columns] = y[:half, here].astype(jnp.bfloat16)
            send_ref[j, :, columns] = y[half:, here].astype(jnp.bfloat16)

    stream(units, ready_ref.shape[0], copies, ahead, prepare, compute)


def gate_up(
    place, blocks, gate_weight, up_weight, ready, unit, start, units, after, has_next, ride=None
):
    rows, depth = blocks[0].shape
    total = rows * len(blocks)
    cols = units * unit
    rides = [] if ride is None else [ride]
    vmem = pl.BlockSpec(memory_space=pltpu.VMEM)
    outs = [jax.ShapeDtypeStruct((2, total // 2, cols), jnp.bfloat16)] * 2
    outs += [jax.ShapeDtypeStruct(r.shape, r.dtype) for r in rides]
    outs += [jax.ShapeDtypeStruct(ready.shape, ready.dtype)] * has_next
    return pl.pallas_call(
        functools.partial(gate_up_kernel, len(blocks), len(rides), has_next, start, units),
        in_specs=[pl.BlockSpec(memory_space=pltpu.SMEM)]
        + [vmem] * len(blocks)
        + [pl.BlockSpec(memory_space=pltpu.HBM)] * 2
        + [vmem] * (1 + len(rides))
        + [pl.BlockSpec(memory_space=pl.ANY)] * len(after),
        out_specs=[vmem] * len(outs),
        out_shape=outs,
        scratch_shapes=[
            pltpu.VMEM((total, depth), jnp.bfloat16),
            pltpu.VMEM((SLOTS, depth, 2 * unit), jnp.bfloat16),
            pltpu.SemaphoreType.DMA((SLOTS, 2)),
            pltpu.SemaphoreType.DMA((READY, 2)),
        ],
        compiler_params=pltpu.CompilerParams(vmem_limit_bytes=VMEM),
        cost_estimate=pl.CostEstimate(
            flops=4 * total * depth * cols,
            bytes_accessed=4 * depth * cols + 2 * total * depth + 4 * total * cols,
            transcendentals=0,
        ),
    )(place, *blocks, gate_weight, up_weight, ready, *rides, *after)


def nothing(*refs):
    pass


def hold(x, after):
    anywhere = pl.BlockSpec(memory_space=pl.ANY)
    return pl.pallas_call(
        nothing,
        in_specs=[anywhere] * (1 + len(after)),
        out_specs=anywhere,
        out_shape=jax.ShapeDtypeStruct(x.shape, x.dtype),
        input_output_aliases={0: 0},
        compiler_params=pltpu.CompilerParams(vmem_limit_bytes=SMALL_VMEM),
        cost_estimate=pl.CostEstimate(flops=0, bytes_accessed=0, transcendentals=0),
    )(x, *after)


def pass_on_kernel(shard, has_flow, own_ref, other_ref, *refs):
    out_ref = refs[-1]
    rows = out_ref.shape[1]
    here = slice(shard * rows, (shard + 1) * rows)
    total = own_ref[:, here].astype(jnp.float32) + other_ref[:, here].astype(jnp.float32)
    if has_flow:
        total = total + refs[0][...].astype(jnp.float32)
    out_ref[...] = total.astype(jnp.bfloat16)


def pass_on(shard, shards, own, other, flow, after):
    vmem = pl.BlockSpec(memory_space=pltpu.VMEM)
    flows = [] if flow is None else [flow]
    return pl.pallas_call(
        functools.partial(pass_on_kernel, shard, len(flows)),
        in_specs=[vmem] * (2 + len(flows)) + [pl.BlockSpec(memory_space=pl.ANY)] * len(after),
        out_specs=vmem,
        out_shape=jax.ShapeDtypeStruct(
            (2, own.shape[1] // shards, own.shape[2]), jnp.bfloat16
        ),
        compiler_params=pltpu.CompilerParams(vmem_limit_bytes=SMALL_VMEM),
        cost_estimate=pl.CostEstimate(
            flops=2 * own.size // shards, bytes_accessed=8 * own.size // shards, transcendentals=0
        ),
    )(own, other, *flows, *after)


def hidden_kernel(n_squares, width, place_ref, flow_ref, own_ref, other_ref, *refs):
    squares, out_ref, all_ref = refs[:n_squares], refs[-2], refs[-1]
    rows = flow_ref.shape[1]
    for i, square in enumerate(squares):
        all_ref[i * square.shape[0] : (i + 1) * square.shape[0]] = square[...]
    here = pl.ds(pl.multiple_of(place_ref[place_ref.shape[0] - 1] * rows, rows), rows)
    inverse = lax.rsqrt(all_ref[here, :] / width + 1e-05)
    gate, up = [
        (
            own_ref[i, -rows:].astype(jnp.float32)
            + other_ref[i, -rows:].astype(jnp.float32)
            + flow_ref[i].astype(jnp.float32)
        )
        * inverse
        for i in range(2)
    ]
    out_ref[...] = (gate / (1 + jnp.exp(-gate)) * up).astype(jnp.bfloat16)


def hidden_units(place, flow, own, other, squares, after):
    _, rows, cols = flow.shape
    vmem = pl.BlockSpec(memory_space=pltpu.VMEM)
    return pl.pallas_call(
        functools.partial(hidden_kernel, len(squares), D),
        in_specs=[pl.BlockSpec(memory_space=pltpu.SMEM)]
        + [vmem] * (3 + len(squares))
        + [pl.BlockSpec(memory_space=pl.ANY)] * len(after),
        out_specs=vmem,
        out_shape=jax.ShapeDtypeStruct((rows, cols), jnp.bfloat16),
        scratch_shapes=[pltpu.VMEM((len(squares) * squares[0].shape[0], 1), jnp.float32)],
        compiler_params=pltpu.CompilerParams(vmem_limit_bytes=SMALL_VMEM),
        cost_estimate=pl.CostEstimate(
            flops=16 * rows * cols, bytes_accessed=14 * rows * cols, transcendentals=rows * cols
        ),
    )(place, flow, own, other, *squares, *after)


def join_kernel(n_shards, *refs):
    out_ref = refs[-1]
    rows = refs[0].shape[0]
    for i, shard in enumerate(refs[:n_shards]):
        out_ref[i * rows : (i + 1) * rows] = shard[...]


def join(shards, after):
    rows, cols = shards[0].shape
    vmem = pl.BlockSpec(memory_space=pltpu.VMEM)
    return pl.pallas_call(
        functools.partial(join_kernel, len(shards)),
        in_specs=[vmem] * len(shards) + [pl.BlockSpec(memory_space=pl.ANY)] * len(after),
        out_specs=vmem,
        out_shape=jax.ShapeDtypeStruct((rows * len(shards), cols), jnp.bfloat16),
        compiler_params=pltpu.CompilerParams(vmem_limit_bytes=SMALL_VMEM),
        cost_estimate=pl.CostEstimate(
            flops=0, bytes_accessed=4 * rows * len(shards) * cols, transcendentals=0
        ),
    )(*shards, *after)


def down_kernel(has_total, n_outs, first_unit, units, place_ref, *refs):
    ours_ref, theirs_ref, weight_ref, ready_ref = refs[:4]
    is_last = n_outs > 2
    x_ref, held, sems, next_sems, *rest = refs[len(refs) - 4 - is_last :]
    outs = refs[len(refs) - 4 - is_last - n_outs : len(refs) - 4 - is_last]
    total_ref = rest[0] if is_last else outs[0]
    half = ours_ref.shape[0]
    unit = held.shape[1]
    ahead = [] if is_last else tiles((weight_ref,), outs[1], next_sems, first_unit + units, True)

    def copies(i, slot):
        here = pl.ds(pl.multiple_of((first_unit + i) * unit, unit), unit)
        return [pltpu.make_async_copy(weight_ref.at[here, :], held.at[slot], sems.at[slot])]

    def prepare():
        x_ref[:half] = ours_ref[...]
        x_ref[half:] = theirs_ref[...]
        total_ref[...] = refs[4][...] if has_total else jnp.zeros_like(total_ref)

    def compute(i, slot):
        columns = pl.ds(i * unit if slot is None else pl.multiple_of(i * unit, unit), unit)
        weight = ready_ref[i] if slot is None else held[slot]
        total_ref[...] += jnp.dot(x_ref[:, columns], weight, preferred_element_type=jnp.float32)

    stream(units, ready_ref.shape[0], copies, ahead, prepare, compute)
    if is_last:
        parts = (place_ref.shape[0] - 1) // n_outs
        for i in range(n_outs * parts):
            out_ref = outs[i // parts]
            rows = out_ref.shape[0] // parts
            term = total_ref[pl.ds(pl.multiple_of(place_ref[i] * rows, rows), rows), :]
            out_ref[i % parts * rows : (i % parts + 1) * rows, :] = term.astype(out_ref.dtype)


def down(place, groups, ours, theirs, weight, ready, total, unit, start, units, after, is_last):
    half, cols = ours.shape
    width = weight.shape[1]
    has_total = total is not None
    vmem = pl.BlockSpec(memory_space=pltpu.VMEM)
    rows = 2 * half // groups
    outs = [
        jax.ShapeDtypeStruct((2 * half, width), jnp.float32),
        jax.ShapeDtypeStruct(ready.shape, ready.dtype),
    ]
    if is_last:
        outs = [jax.ShapeDtypeStruct((rows, width), jnp.float32)]
        outs += [jax.ShapeDtypeStruct((rows, width), jnp.bfloat16)] * (groups - 1)
    return pl.pallas_call(
        functools.partial(down_kernel, has_total, len(outs), start, units),
        in_specs=[pl.BlockSpec(memory_space=pltpu.SMEM), vmem, vmem]
        + [pl.BlockSpec(memory_space=pltpu.HBM), vmem]
        + [vmem] * has_total
        + [pl.BlockSpec(memory_space=pl.ANY)] * len(after),
        out_specs=[vmem] * len(outs),
        out_shape=outs,
        scratch_shapes=[
            pltpu.VMEM((2 * half, cols), jnp.bfloat16),
            pltpu.VMEM((SLOTS, unit, width), jnp.bfloat16),
            pltpu.SemaphoreType.DMA((SLOTS,)),
            pltpu.SemaphoreType.DMA((READY_DOWN, 1)),
        ]
        + [pltpu.VMEM((2 * half, width), jnp.float32)] * is_last,
        compiler_params=pltpu.CompilerParams(vmem_limit_bytes=VMEM),
        cost_estimate=pl.CostEstimate(
            flops=4 * half * units * unit * width,
            bytes_accessed=2 * units * unit * width + 16 * half * width,
            transcendentals=0,
        ),
    )(place, ours, theirs, weight, ready, *([total] if has_total else []), *after)


def attend(residual_in, queries, key_cache, value_cache, key_new, value_new, lengths):
    cycle_size = lax.axis_size("blk")
    quarters = cycle_size // KV_HEADS
    per_kv = HEADS // KV_HEADS
    own_heads = HEADS // cycle_size
    head_size = key_cache.shape[3]
    seq_rows = residual_in.shape[0]
    positions_here = key_cache.shape[2]
    blk_index = lax.axis_index("blk")
    kv_head = blk_index // quarters
    quarter = blk_index % quarters
    score_scale = 1.0 / math.sqrt(head_size)
    group_queries = lax.dynamic_slice_in_dim(
        queries, kv_head * per_kv * head_size, per_kv * head_size, 1
    )
    group_queries = group_queries.astype(jnp.float32).reshape(seq_rows, per_kv, head_size)
    fresh_key = lax.dynamic_slice_in_dim(key_new, kv_head * head_size, head_size, 1).astype(
        jnp.float32
    )
    fresh_value = lax.dynamic_slice_in_dim(value_new, kv_head * head_size, head_size, 1).astype(
        jnp.float32
    )
    keys_here = key_cache[:, 0].astype(jnp.float32)
    values_here = value_cache[:, 0].astype(jnp.float32)
    scores = jnp.einsum("shd,spd->shp", group_queries, keys_here) * score_scale
    fresh_scores = jnp.einsum("shd,sd->sh", group_queries, fresh_key) * score_scale
    places = quarter * positions_here + jnp.arange(positions_here, dtype=jnp.int32)
    usable = (places[None, :] < lengths[:, None])[:, None, :]
    with_fresh = quarter == 0
    largest = jnp.maximum(
        jnp.max(jnp.where(usable, scores, -1e30), axis=2),
        jnp.where(with_fresh, fresh_scores, -1e30),
    )
    weights = jnp.where(usable, jnp.exp(scores - largest[..., None]), 0.0)
    fresh_weight = jnp.where(with_fresh, jnp.exp(fresh_scores - largest), 0.0)
    totals = jnp.sum(weights, axis=2) + fresh_weight
    weighted = (
        jnp.einsum("shp,spd->shd", weights, values_here)
        + fresh_weight[..., None] * fresh_value[:, None, :]
    )
    for bit_number in range(quarters.bit_length() - 1):
        peer_max, peer_total, peer_weighted = partner(
            (largest, totals, weighted), "blk", 1 << bit_number
        )
        merged = jnp.maximum(largest, peer_max)
        mine_factor = jnp.exp(largest - merged)
        peer_factor = jnp.exp(peer_max - merged)
        totals = totals * mine_factor + peer_total * peer_factor
        weighted = weighted * mine_factor[..., None] + peer_weighted * peer_factor[..., None]
        largest = merged
    attention = weighted / totals[..., None]
    own_output = lax.dynamic_slice_in_dim(attention, quarter * own_heads, own_heads, 1).reshape(
        seq_rows, own_heads * head_size
    )
    return residual_in.astype(jnp.float32) + own_output


def on_device(
    residual_in,
    queries,
    key_cache,
    value_cache,
    key_new,
    value_new,
    lengths,
    ffn_gain,
    gate_weight,
    up_weight,
    down_weight,
):
    groups = lax.axis_size("grp")
    group = lax.axis_index("grp")
    chips = lax.axis_size("blk") // 2
    chip, core = lax.axis_index("blk") // 2, lax.axis_index("blk") % 2
    rows = residual_in.shape[0]
    parts = 2 * chips // groups

    wide = attend(residual_in, queries, key_cache, value_cache, key_new, value_new, lengths)

    tokens = (wide * ffn_gain.astype(jnp.float32)[None, :]).astype(jnp.bfloat16)
    blocks = [tokens] + [partner(tokens, "grp", i) for i in range(1, groups)]

    squares = jnp.sum(wide * wide, axis=1, keepdims=True)
    for bit_number in range(lax.axis_size("blk").bit_length() - 1):
        squares = squares + partner(squares, "blk", 1 << bit_number)

    spot = jnp.where(chip % 2 == 1, (chip + 1) // 2, (chips - chip // 2) % chips)
    shard = jnp.arange(groups * parts, dtype=jnp.int32) ^ (group * parts)
    place = (spot - 1 - shard) % chips + jnp.where(shard // chips == core, 0, chips)
    own_shard = (core * chips + spot) ^ (group * parts)
    place = jnp.concatenate([place, own_shard[None]]).astype(jnp.int32)

    unit = gate_weight.shape[1] // sum(CHUNK_UNITS)
    edges = [sum(CHUNK_UNITS[:i]) for i in range(len(CHUNK_UNITS) + 1)]
    f32 = jnp.float32
    n_chunks = len(CHUNK_UNITS)
    total = None
    chunks = [{} for _ in range(n_chunks)]
    shape = (READY, tokens.shape[1], 2 * unit)
    ready = bring((gate_weight, up_weight), shape, 0, False, [tokens])
    last = [ready]

    def turn_of(k, stage):
        return k + stage - (k == 0 and stage > 0)

    flowing = [0, 2 * chips, *range(1, chips + 1), None, 2 * chips - 1]
    closing = [None, 2 * chips, 2 * chips - 1]
    for turn in range(n_chunks + 2 * chips):
        if turn == n_chunks + 1:
            shape = (READY_DOWN, 2 * unit, down_weight.shape[1])
            ready = bring((down_weight,), shape, 0, True, last)
            last = [ready]
        for stage in flowing if turn < n_chunks + chips else closing:
            if stage is None:
                for k in range(n_chunks):
                    for j in range(1, chips - 1):
                        if turn_of(k, chips + j) == turn:
                            hidden = hold(chunks[k]["hidden"][j], last)
                            last = [hidden]
                            chunks[k]["hidden"][j] = hidden
                            chunks[k]["hidden"].append(along_ring(hidden))
                if turn == 1:
                    last = last + squares
                continue
            for k in range(n_chunks):
                if turn_of(k, stage) != turn:
                    continue
                units, chunk = CHUNK_UNITS[k], chunks[k]
                is_last = k == n_chunks - 1
                if stage == 0:
                    ride = squares if k == 0 else None
                    keep, send, *rest = gate_up(
                        place, blocks, gate_weight, up_weight, ready, unit, edges[k], units, last,
                        not is_last, ride,
                    )
                    ready = rest[-1] if rest else None
                    last = [keep]
                    chunk.update(own=keep, flow=None)
                    if k == 0:
                        chunk["other"] = partner(send, "blk", 1)
                        squares = [rest[0]] + [partner(rest[0], "grp", i) for i in range(1, groups)]
                elif stage < chips:
                    flow = pass_on(
                        stage - 1, chips, chunk["own"], chunk["other"], chunk["flow"], last
                    )
                    last = [flow]
                    chunk["flow"] = along_ring(flow)
                elif stage == chips:
                    hidden = hidden_units(
                        place, chunk["flow"], chunk["own"], chunk["other"], squares, last
                    )
                    last = [hidden]
                    chunk["hidden"] = [hidden, along_ring(hidden)]
                elif stage == 2 * chips - 1:
                    ours = join(chunk["hidden"][1:] + chunk["hidden"][:1], last)
                    last = [ours]
                    chunk.update(ours=ours, theirs=partner(ours, "blk", 1))
                else:
                    total, *terms = down(
                        place, groups, chunk["ours"], chunk["theirs"], down_weight, ready, total,
                        2 * unit, edges[k] // 2, units // 2, last, is_last,
                    )
                    ready = terms[0]
                    last = [total]
        if 0 < turn < n_chunks:
            send = hold(send, last)
            last = [send]
            chunks[turn]["other"] = partner(send, "blk", 1)

    out = wide + total
    for i in range(1, groups):
        out = out + partner(terms[i - 1], "grp", i).astype(f32)
    return out


def solution(mesh):
    in_specs = (
        P("grp", "blk"),
        P("grp", None),
        P("grp", "blk", None, None),
        P("grp", "blk", None, None),
        P("grp", None),
        P("grp", None),
        P("grp"),
        P("blk"),
        P("blk", "grp"),
        P("blk", "grp"),
        P("grp", "blk"),
    )
    out_specs = P("grp", "blk")
    return jax.shard_map(
        on_device, mesh=mesh, in_specs=in_specs, out_specs=out_specs, check_vma=False
    )
```
